32 devices in a mesh: dp: 8 (over z, x), fsdp: 4 (over y, core).
Axes of the slice: x: 2, y: 2, z: 4, core: 2. Of those that a mesh axis runs over, the one named last changes fastest.
Arguments:
- queries: bfloat16 [4, 16, 128, 2048], P('fsdp', 'dp'), may hold values from -6 to 6
- response_key_value: bfloat16 [4, 16, 128, 2048], P('fsdp', 'dp'), may hold values from -6 to 6
- prompt_kv: bfloat16 [4, 1024, 2048], P('fsdp', 'dp'), may hold values from -6 to 6
- out_weight: bfloat16 [2048, 4608], P(None, 'fsdp'), may hold values from -0.125 to 0.125
- residual: bfloat16 [4, 16, 128, 4608], P('fsdp', 'dp'), may hold values from -6 to 6
- post_gain: float32 [4608], replicated, may hold values from 0.1 to 1.9
- final_gain: float32 [4608], replicated, may hold values from 0.1 to 1.9
- target_rows: bfloat16 [4, 16, 128, 4608], P('fsdp', 'dp'), may hold values from -0.046875 to 0.046875
- log_norm: float32 [4, 16, 128], P('fsdp', 'dp'), may hold values from 9.5 to 10.5
- old_logp: float32 [4, 16, 128], P('fsdp', 'dp'), may hold values from -10.5 to -9.5
- ref_logp: float32 [4, 16, 128], P('fsdp', 'dp'), may hold values from -10.5 to -9.5
- lengths: int32 [4, 16], P('fsdp', 'dp'), may hold values from 1 to 128, 682 in all within a row
- rewards: float32 [4, 16], P('fsdp', 'dp'), may hold values from -4 to 4
Outputs:
- log_ratio: float32 [4, 16, 128], P('fsdp', 'dp')
- kl_terms: float32 [4, 16, 128], P('fsdp', 'dp')
- objective: float32 [4, 16, 128], P('fsdp', 'dp')
- batch_loss: float32 [], replicated
The draws below stay inside these ranges and needn't reach their ends.
Inputs may be any that keep to these rules, and one draw needn't show every extreme that they name: The 16 lengths of each prompt sum to 682, and the largest of each prompt is exactly 128.
All inputs are finite; a program needn't handle non-finite values.
Results may differ from the reference program's by a relative error of at most 0.0033.
Values may be sent and summed in bfloat16 or wider, within the bound.
No kernel may reach another device: no remote copies, remote signals or barrier semaphores. Data moves between devices by JAX's collectives and lax.ppermute only.
A program may use at most 128 MiB of HBM per device.

```python
import math
import jax
import jax.numpy as jnp
import numpy as np
from jax import lax

D = 4608
QUERY_HEADS = 16
KEY_VALUE_HEADS = 8
HEAD_SIZE = 128
QPRE = 144
PROMPT_LENGTH = 1024
LMAX = 128
QD = 2048
KVD = 1024
PROMPTS = 4
GROUP = 16


def shard_levels(rng, shape, cuts, low, high):
    level = 1.0
    for dim, parts in cuts:
        heights = jax.random.uniform(jax.random.fold_in(jax.random.fold_in(rng, 6), dim), (parts,), jnp.float32, low / len(cuts), high / len(cuts))
        level = level * jnp.repeat(jnp.exp(heights), shape[dim] // parts).reshape((-1,) + (1,) * (len(shape) - 1 - dim))
    return level


def split_up(count, total, bound, lean):
    weights = [(1 << 20) // math.isqrt(grade ** lean) + 1 for grade in range(2, count + 1)]
    spare, holding = total - bound - (count - 1), [1] * (count - 1)
    while spare > 0:
        movable = [i for i in range(count - 1) if holding[i] < bound]
        whole, left = sum([weights[i] for i in movable]), spare
        for i in movable:
            more = min(bound - holding[i], max(1, left * weights[i] // whole), spare)
            holding[i] = holding[i] + more
            spare = spare - more
    return np.array([bound] + holding)


def ragged(own_key, count, total, bound, slope):
    if count == 2:
        one = jax.random.randint(own_key, (), max(1, total - bound), min(bound, total - 1) + 1)
        return jnp.stack([one, total - one])
    sizes = jnp.asarray(split_up(count, total, bound, slope), jnp.int32)
    twos = (count - 1) // 2
    donor, sink = sizes[1:1 + 2 * twos:2], sizes[2:2 + 2 * twos:2]
    room = jnp.minimum(donor - 1, bound - sink)
    passed = jax.random.randint(jax.random.fold_in(own_key, 1), (twos,), 0, 1 << 20) % (room + 1)
    sizes = sizes.at[1:1 + 2 * twos:2].set(donor - passed).at[2:2 + 2 * twos:2].set(sink + passed)
    return sizes[jax.random.permutation(jax.random.fold_in(own_key, 2), count)]


def normal_values(rng, extent, scale, reach, cuts=(), held_as=jnp.bfloat16):
    array = jax.random.normal(rng, extent, jnp.float32) * scale
    if len(cuts) > 0:
        array = shard_levels(rng, extent, cuts, -0.22, 0.18) * array
    return jnp.clip(array, min=-reach, max=reach).astype(held_as)


def setup_inputs(seed: int = 0) -> dict:
    splits = jax.random.split(jax.random.key(seed), 14)
    queries = normal_values(splits[0], (PROMPTS, GROUP, LMAX, QD), 1.0, 6.0, ((0, 4), (1, 8)))
    response_key_value = normal_values(splits[1], (PROMPTS, GROUP, LMAX, 2 * KVD), 1.0, 6.0, ((0, 4), (1, 8)))
    prompt_kv = normal_values(splits[2], (PROMPTS, PROMPT_LENGTH, 2 * KVD), 1.0, 6.0, ((0, 4), (1, 8)))
    out_weight = normal_values(splits[3], (QD, D), QD ** -0.5, 0.125, ((1, 4),))
    residual = normal_values(splits[4], (PROMPTS, GROUP, LMAX, D), 1.0, 6.0, ((0, 4), (1, 8)))
    post_gain = jnp.clip(1.0 + 0.18 * jax.random.normal(splits[5], (D,), jnp.float32), 0.1, 1.9)
    final_gain = jnp.clip(1.0 + 0.18 * jax.random.normal(splits[6], (D,), jnp.float32), 0.1, 1.9)
    target_rows = normal_values(splits[7], (PROMPTS, GROUP, LMAX, D), (4 * D) ** -0.5, 0.046875, ((0, 4), (1, 8)))
    log_norm = jnp.clip(9.5 + 1.0 * jax.random.uniform(splits[8], (PROMPTS, GROUP, LMAX), jnp.float32) ** shard_levels(splits[8], (PROMPTS, GROUP, LMAX), ((0, 4), (1, 8)), -0.2, 0.2), 9.5, 10.5)
    old_logp = jnp.clip(-10.5 + 1.0 * jax.random.uniform(splits[9], (PROMPTS, GROUP, LMAX), jnp.float32) ** shard_levels(splits[9], (PROMPTS, GROUP, LMAX), ((0, 4), (1, 8)), -0.2, 0.2), -10.5, -9.5)
    ref_logp = jnp.clip(-10.5 + 1.0 * jax.random.uniform(splits[10], (PROMPTS, GROUP, LMAX), jnp.float32) ** shard_levels(splits[10], (PROMPTS, GROUP, LMAX), ((0, 4), (1, 8)), -0.2, 0.2), -10.5, -9.5)
    lengths = jax.vmap(lambda own: ragged(own, GROUP, GROUP * LMAX // 3, LMAX, 2))(jax.random.split(splits[11], PROMPTS)).reshape((PROMPTS, GROUP)).astype(jnp.int32)
    rewards = normal_values(splits[12], (PROMPTS, GROUP), 1.0, 4.0, ((0, 4), (1, 8)), jnp.float32)
    return dict(queries=queries, response_key_value=response_key_value, prompt_kv=prompt_kv, out_weight=out_weight, residual=residual, post_gain=post_gain, final_gain=final_gain, target_rows=target_rows, log_norm=log_norm, old_logp=old_logp, ref_logp=ref_logp, lengths=lengths, rewards=rewards)


def capped(values, limit):
    return limit * jnp.tanh(values / limit)

def rms_scaled(values, gain):
    mean_square = lax.optimization_barrier(jnp.mean(values * values, axis=-1, keepdims=True))
    return values * lax.rsqrt(mean_square + 1e-06) * gain

def reference(queries, response_key_value, prompt_kv, out_weight, residual, post_gain, final_gain, target_rows, log_norm, old_logp, ref_logp, lengths, rewards):
    per_key_value = QUERY_HEADS // KEY_VALUE_HEADS
    key_value_width = KEY_VALUE_HEADS * HEAD_SIZE
    score_scale = QPRE ** (-0.5)

    def one_prompt(pieces):
        query_matrix_rows, response_rows, prompt_token_rows, stream_rows, target_block = pieces
        group_members = query_matrix_rows.shape[0]
        token_positions = query_matrix_rows.shape[1]
        query_result = query_matrix_rows.astype(jnp.float32).reshape(group_members, token_positions, KEY_VALUE_HEADS, per_key_value, HEAD_SIZE)
        key_matrix_rows = prompt_token_rows[:, :key_value_width].astype(jnp.float32).reshape(PROMPT_LENGTH, KEY_VALUE_HEADS, HEAD_SIZE)
        value_matrix_rows = prompt_token_rows[:, key_value_width:].astype(jnp.float32).reshape(PROMPT_LENGTH, KEY_VALUE_HEADS, HEAD_SIZE)
        scores = capped(jnp.einsum('glkhd,nkd->glkhn', query_result, key_matrix_rows) * score_scale, 50.0)
        weights = jnp.exp(scores)
        rounded = lax.optimization_barrier(weights.astype(jnp.bfloat16)).astype(jnp.float32)
        numerator = jnp.einsum('glkhn,nkd->glkhd', rounded, value_matrix_rows)
        denominator = lax.optimization_barrier(jnp.sum(weights, axis=-1))
        response_keys = response_rows[..., :key_value_width].astype(jnp.float32).reshape(group_members, token_positions, KEY_VALUE_HEADS, HEAD_SIZE)
        response_values = response_rows[..., key_value_width:].astype(jnp.float32).reshape(group_members, token_positions, KEY_VALUE_HEADS, HEAD_SIZE)
        own_scores = capped(jnp.einsum('glkhd,gmkd->glkhm', query_result, response_keys) * score_scale, 50.0)
        later = lax.broadcasted_iota(jnp.int32, (token_positions, token_positions), 0)
        earlier = lax.broadcasted_iota(jnp.int32, (token_positions, token_positions), 1)
        causal = (earlier <= later)[None, :, None, None, :]
        own_weights = jnp.where(causal, jnp.exp(own_scores), 0.0)
        own_rounded = lax.optimization_barrier(own_weights.astype(jnp.bfloat16)).astype(jnp.float32)
        numerator = numerator + jnp.einsum('glkhm,gmkd->glkhd', own_rounded, response_values)
        denominator = denominator + lax.optimization_barrier(jnp.sum(own_weights, axis=-1))
        attended = (numerator / denominator[..., None]).astype(jnp.bfloat16).reshape(group_members * token_positions, QUERY_HEADS * HEAD_SIZE)
        projected = jnp.dot(attended, out_weight, preferred_element_type=jnp.float32)
        mixed = stream_rows.reshape(group_members * token_positions, D).astype(jnp.float32) + rms_scaled(projected, post_gain)
        hidden = rms_scaled(mixed, final_gain)
        logit = capped(lax.optimization_barrier(jnp.sum(hidden * target_block.reshape(group_members * token_positions, D).astype(jnp.float32), axis=-1)), 30.0)
        return logit.reshape(group_members, token_positions)
    logits = lax.map(one_prompt, (queries, response_key_value, prompt_kv, residual, target_rows))
    logp = logits - log_norm
    position_ids = lax.broadcasted_iota(jnp.int32, logp.shape, 2)
    live_mask = position_ids < lengths[:, :, None]
    log_ratio = jnp.where(live_mask, logp - old_logp, 0.0)
    drift = ref_logp - logp
    kl_terms = jnp.where(live_mask, jnp.exp(drift) - drift - 1.0, 0.0)
    advantage = rewards - lax.optimization_barrier(jnp.mean(rewards, axis=1, keepdims=True))
    prob_ratio = jnp.exp(logp - old_logp)
    surrogate = jnp.minimum(prob_ratio * advantage[:, :, None], jnp.clip(prob_ratio, 0.8, 1.2) * advantage[:, :, None])
    objective = jnp.where(live_mask, 0.04 * kl_terms - surrogate, 0.0)
    batch_loss = jnp.sum(objective) / jnp.sum(live_mask.astype(jnp.float32))
    return (log_ratio, kl_terms, objective, batch_loss)
```

```python
import functools
import math

import jax
import jax.numpy as jnp
from jax import lax
from jax.experimental import pallas as pl
from jax.experimental.pallas import tpu as pltpu
from jax.sharding import PartitionSpec as P

D = 4608
KEY_VALUE_HEADS = 8
PER_KEY_VALUE = 2
HEAD_SIZE = 128
QPRE = 144
GROUPS = 2
SUMS = 8


def swap(value, axis, bit):
    count = lax.axis_size(axis)
    return lax.ppermute(value, axis, [(i, i ^ bit) for i in range(count)])


def around(value, axis):
    half = lax.axis_size(axis) // 2
    order = list(range(0, half, 2)) + list(range(1, half, 2))[::-1]
    after = {order[i]: order[(i + 1) % half] for i in range(half)}
    return lax.ppermute(
        value, axis, [(i, after[i // 2] * 2 + i % 2) for i in range(2 * half)]
    )


def attention_kernel(count, q_ref, rk_ref, rv_ref, *refs):
    key_refs, value_refs, out_ref = refs[:count], refs[count : 2 * count], refs[-1]
    responses, length, _ = q_ref.shape
    tokens = responses * length
    inner = QPRE**-0.5 / 50.0
    outer = 50.0 * math.log2(math.e)
    q = q_ref[...].reshape(tokens, PER_KEY_VALUE * HEAD_SIZE)
    heads = [q[:, h * HEAD_SIZE : (h + 1) * HEAD_SIZE] for h in range(PER_KEY_VALUE)]
    keys = jnp.concatenate([ref[...] for ref in key_refs], axis=0)
    values = jnp.concatenate([ref[...] for ref in value_refs], axis=0)
    later = lax.broadcasted_iota(jnp.int32, (length, length), 0)
    earlier = lax.broadcasted_iota(jnp.int32, (length, length), 1)
    causal = earlier <= later
    chunk = 256

    def weigh(q_rows, k_rows):
        scores = lax.dot_general(
            q_rows, k_rows, (((1,), (1,)), ((), ())), preferred_element_type=jnp.float32
        )
        return jnp.exp2(outer * jnp.tanh(scores * inner))

    for h in range(PER_KEY_VALUE):
        for r in range(responses):
            rows = heads[h][r * length : (r + 1) * length]
            own = jnp.where(causal, weigh(rows, rk_ref[r]), 0.0)
            total = own
            numerator = jnp.dot(
                own.astype(jnp.bfloat16), rv_ref[r], preferred_element_type=jnp.float32
            )
            for start in range(0, keys.shape[0], chunk):
                weights = weigh(rows, keys[start : start + chunk])
                for lane in range(0, chunk, HEAD_SIZE):
                    total = total + weights[:, lane : lane + HEAD_SIZE]
                numerator = numerator + jnp.dot(
                    weights.astype(jnp.bfloat16),
                    values[start : start + chunk],
                    preferred_element_type=jnp.float32,
                )
            denominator = jnp.sum(total, axis=-1, keepdims=True)
            out_ref[r * length : (r + 1) * length, h * HEAD_SIZE : (h + 1) * HEAD_SIZE] = (
                numerator / denominator
            ).astype(jnp.bfloat16)


def attend(queries, response_key_value, blocks, group):
    responses, length, _ = queries.shape
    per_group = KEY_VALUE_HEADS // GROUPS
    count = len(blocks)
    rows = blocks[0].shape[0]
    width = PER_KEY_VALUE * HEAD_SIZE
    first = group * per_group
    in_specs = [
        pl.BlockSpec((responses, length, width), lambda i: (0, 0, first + i)),
        pl.BlockSpec((responses, length, HEAD_SIZE), lambda i: (0, 0, first + i)),
        pl.BlockSpec((responses, length, HEAD_SIZE), lambda i: (0, 0, KEY_VALUE_HEADS + first + i)),
    ]
    in_specs += [pl.BlockSpec((rows, HEAD_SIZE), lambda i: (0, i))] * count
    in_specs += [pl.BlockSpec((rows, HEAD_SIZE), lambda i: (0, per_group + i))] * count
    tokens = responses * length
    return pl.pallas_call(
        functools.partial(attention_kernel, count),
        grid=(per_group,),
        in_specs=in_specs,
        out_specs=pl.BlockSpec((tokens, width), lambda i: (0, i)),
        out_shape=jax.ShapeDtypeStruct((tokens, per_group * width), jnp.bfloat16),
        compiler_params=pltpu.CompilerParams(vmem_limit_bytes=32 * 1024 * 1024),
        cost_estimate=pl.CostEstimate(
            flops=2 * 2 * tokens * 2 * per_group * 1152 * 128,
            bytes_accessed=4 * 1024 * 1024,
            transcendentals=2 * tokens * 2 * per_group * 1152,
        ),
    )(queries, response_key_value, response_key_value, *blocks, *blocks)


def project_kernel(sources, weight_ref, gain_ref, *refs):
    out_ref = refs[-1]
    post = gain_ref[0:1, :]
    final = gain_ref[1:2, :]
    part = weight_ref.shape[0] // GROUPS
    for s in range(sources):
        tail_ref = refs[s * (GROUPS + 1)]
        attended = [refs[s * (GROUPS + 1) + 1 + g] for g in range(GROUPS)]
        tokens = attended[0].shape[0]
        projected = jnp.dot(
            attended[0][...], weight_ref[0:part, :], preferred_element_type=jnp.float32
        )
        for g in range(1, GROUPS):
            projected += jnp.dot(
                attended[g][...],
                weight_ref[g * part : (g + 1) * part, :],
                preferred_element_type=jnp.float32,
            )
        residual = tail_ref[0:tokens, :].astype(jnp.float32)
        target = tail_ref[tokens : 2 * tokens, :].astype(jnp.float32) * final
        scaled = projected * post
        lane = lax.broadcasted_iota(jnp.int32, (tokens, 128), 1)
        packed = jnp.zeros((tokens, 128), jnp.float32)
        terms = (
            projected * projected,
            residual * scaled,
            scaled * scaled,
            target * scaled,
            residual * residual,
            residual * target,
        )
        for k, term in enumerate(terms):
            packed = jnp.where(lane == k, jnp.sum(term, axis=-1, keepdims=True), packed)
        out_ref[s] = jnp.transpose(packed)[0:SUMS, :]


def project(weight, gains, tails, attended):
    sources = len(tails)
    tokens = attended[0][0].shape[0]
    width = weight.shape[1]
    operands = [weight, gains]
    for s in range(sources):
        operands += [tails[s]] + list(attended[s])
    return pl.pallas_call(
        functools.partial(project_kernel, sources),
        out_shape=jax.ShapeDtypeStruct((sources, SUMS, tokens), jnp.float32),
        compiler_params=pltpu.CompilerParams(vmem_limit_bytes=48 * 1024 * 1024),
        cost_estimate=pl.CostEstimate(
            flops=2 * sources * tokens * 2048 * width,
            bytes_accessed=8 * 1024 * 1024,
            transcendentals=0,
        ),
    )(*operands)


def body(
    queries,
    response_key_value,
    prompt_kv,
    out_weight,
    residual,
    post_gain,
    final_gain,
    target_rows,
    log_norm,
    old_logp,
    ref_logp,
    lengths,
    rewards,
):
    _, responses, length, _ = queries.shape
    tokens = responses * length
    fsdp = lax.axis_size("fsdp")
    dp = lax.axis_size("dp")
    here = lax.axis_index("fsdp")
    columns = D // fsdp
    key_value_width = KEY_VALUE_HEADS * HEAD_SIZE
    part = key_value_width // GROUPS

    gathered = []
    for g in range(GROUPS):
        block = jnp.concatenate(
            [
                prompt_kv[0, :, g * part : (g + 1) * part],
                prompt_kv[0, :, key_value_width + g * part : key_value_width + (g + 1) * part],
            ],
            axis=1,
        )
        blocks = [block, swap(block, "dp", 1)]
        for _ in range(dp // 2 - 1):
            block = around(block, "dp")
            blocks += [block, swap(block, "dp", 1)]
        gathered.append(blocks)

    tail = jnp.concatenate(
        [residual[0].reshape(tokens, D), target_rows[0].reshape(tokens, D)], axis=0
    )
    tails = []
    for k in range(fsdp):
        piece = lax.dynamic_slice_in_dim(tail, (here ^ k) * columns, columns, 1)
        tails.append(swap(piece, "fsdp", k) if k else piece)
    gains = lax.dynamic_slice_in_dim(
        jnp.stack([post_gain, final_gain]), here * columns, columns, 1
    )

    sums = jnp.stack([jnp.sum(rewards[0]), jnp.sum(lengths[0]).astype(jnp.float32)])
    sums = jnp.pad(sums[None], ((0, 0), (0, 126)))
    bit = 1
    while bit < dp:
        sums = sums + swap(sums, "dp", bit)
        bit *= 2
    meta = jnp.concatenate(
        [sums[0, :2], rewards[0], lengths[0].astype(jnp.float32)]
    )
    meta = jnp.pad(meta[None], ((0, 0), (0, length - meta.shape[0])))
    facts = [jnp.concatenate([log_norm[0], old_logp[0], ref_logp[0], meta], axis=0)]
    bit = 1
    while bit < fsdp:
        facts = facts + [swap(value, "fsdp", bit) for value in facts]
        bit *= 2
    facts = jnp.stack(facts)

    attended = [[None] * GROUPS for _ in range(fsdp)]
    for g in range(GROUPS):
        attended[0][g] = attend(queries[0], response_key_value[0], gathered[g], g)
        bit = fsdp // 2
        known = [0]
        while bit:
            for k in known:
                attended[k ^ bit][g] = swap(attended[k][g], "fsdp", bit)
            known = known + [k ^ bit for k in known]
            bit //= 2

    near = list(range(min(2, fsdp)))
    far = list(range(2, fsdp))
    parts = []
    for some in (near, far):
        parts.append(
            project(out_weight, gains, [tails[k] for k in some], [attended[k] for k in some])
        )
    totals = jnp.concatenate(parts, axis=0)
    bit = 1
    while bit < fsdp:
        other = swap(totals, "fsdp", bit)
        totals = totals + jnp.stack([other[k ^ bit] for k in range(fsdp)])
        bit *= 2

    totals = totals.reshape(fsdp, SUMS, responses, length)
    inverse = lax.rsqrt(totals[:, 0] / D + 1e-06)
    square = totals[:, 4] + inverse * (2.0 * totals[:, 1] + inverse * totals[:, 2])
    outer = lax.rsqrt(jnp.maximum(square, 0.0) / D + 1e-06)
    raw = outer * (totals[:, 5] + inverse * totals[:, 3])
    logit = 30.0 * jnp.tanh(raw / 30.0)
    logp = logit - facts[:, 0:responses]
    old = facts[:, responses : 2 * responses]
    ref = facts[:, 2 * responses : 3 * responses]
    meta = facts[:, 3 * responses]
    group_sum, group_count = meta[:, 0], meta[:, 1]
    reward = meta[:, 2 : 2 + responses]
    size = meta[:, 2 + responses : 2 + 2 * responses].astype(jnp.int32)
    position = lax.broadcasted_iota(jnp.int32, (fsdp, responses, length), 2)
    live = position < size[:, :, None]
    log_ratio = jnp.where(live, logp - old, 0.0)
    drift = ref - logp
    kl_terms = jnp.where(live, jnp.exp(drift) - drift - 1.0, 0.0)
    advantage = (reward - (group_sum / (responses * dp))[:, None])[:, :, None]
    ratio = jnp.exp(logp - old)
    surrogate = jnp.minimum(ratio * advantage, jnp.clip(ratio, 0.8, 1.2) * advantage)
    objective = jnp.where(live, 0.04 * kl_terms - surrogate, 0.0)
    loss = jnp.full((1, 128), jnp.sum(objective))
    bit = 1
    while bit < dp:
        loss = loss + swap(loss, "dp", bit)
        bit *= 2
    batch_loss = loss[0, 0] / jnp.sum(group_count)
    return (log_ratio[:1], kl_terms[:1], objective[:1], batch_loss)


def solution(mesh):
    rows4 = P("fsdp", "dp", None, None)
    rows3 = P("fsdp", "dp", None)
    in_specs = (
        rows4,
        rows4,
        rows3,
        P(None, "fsdp"),
        rows4,
        P(),
        P(),
        rows4,
        rows3,
        rows3,
        rows3,
        P("fsdp", "dp"),
        P("fsdp", "dp"),
    )
    out_specs = (rows3, rows3, rows3, P())
    return jax.shard_map(body, mesh=mesh, in_specs=in_specs, out_specs=out_specs, check_vma=False)
```

```python
import functools
import math

import jax
import jax.numpy as jnp
from jax import lax
from jax.experimental import pallas as pl
from jax.experimental.pallas import tpu as pltpu
from jax.sharding import PartitionSpec as P

D = 4608
KEY_VALUE_HEADS = 8
PER_KEY_VALUE = 2
HEAD_SIZE = 128
QPRE = 144
GROUPS = 2
SUMS = 8


def swap(value, axis, bit):
    count = lax.axis_size(axis)
    return lax.ppermute(value, axis, [(i, i ^ bit) for i in range(count)])


def around(value, axis):
    half = lax.axis_size(axis) // 2
    order = list(range(0, half, 2)) + list(range(1, half, 2))[::-1]
    after = {order[i]: order[(i + 1) % half] for i in range(half)}
    return lax.ppermute(
        value, axis, [(i, after[i // 2] * 2 + i % 2) for i in range(2 * half)]
    )


def attention_kernel(count, q_ref, rk_ref, rv_ref, *refs):
    key_refs, value_refs, out_ref = refs[:count], refs[count : 2 * count], refs[-1]
    responses, length, _ = q_ref.shape
    tokens = responses * length
    inner = QPRE**-0.5 / 50.0
    outer = 50.0 * math.log2(math.e)
    q = q_ref[...].reshape(tokens, PER_KEY_VALUE * HEAD_SIZE)
    heads = [q[:, h * HEAD_SIZE : (h + 1) * HEAD_SIZE] for h in range(PER_KEY_VALUE)]
    keys = jnp.concatenate([ref[...] for ref in key_refs], axis=0)
    values = jnp.concatenate([ref[...] for ref in value_refs], axis=0)
    later = lax.broadcasted_iota(jnp.int32, (length, length), 0)
    earlier = lax.broadcasted_iota(jnp.int32, (length, length), 1)
    causal = earlier <= later
    chunk = 512

    def weigh(q_rows, k_rows):
        scores = lax.dot_general(
            q_rows, k_rows, (((1,), (1,)), ((), ())), preferred_element_type=jnp.float32
        )
        return jnp.exp2(outer * jnp.tanh(scores * inner))

    stack = jnp.concatenate(heads, axis=0)
    owned, numerators = [], []
    for h in range(PER_KEY_VALUE):
        for r in range(responses):
            rows = heads[h][r * length : (r + 1) * length]
            own = jnp.where(causal, weigh(rows, rk_ref[r]), 0.0)
            owned.append(own)
            numerators.append(
                jnp.dot(own.astype(jnp.bfloat16), rv_ref[r], preferred_element_type=jnp.float32)
            )
    total = jnp.concatenate(owned, axis=0)
    numerator = jnp.concatenate(numerators, axis=0)
    for start in range(0, keys.shape[0], chunk):
        weights = weigh(stack, keys[start : start + chunk])
        for lane in range(0, chunk, HEAD_SIZE):
            total = total + weights[:, lane : lane + HEAD_SIZE]
        numerator = numerator + jnp.dot(
            weights.astype(jnp.bfloat16),
            values[start : start + chunk],
            preferred_element_type=jnp.float32,
        )
    result = (numerator / jnp.sum(total, axis=-1, keepdims=True)).astype(jnp.bfloat16)
    for h in range(PER_KEY_VALUE):
        out_ref[:, h * HEAD_SIZE : (h + 1) * HEAD_SIZE] = result[h * tokens : (h + 1) * tokens]


def attend(queries, response_key_value, blocks, group):
    responses, length, _ = queries.shape
    per_group = KEY_VALUE_HEADS // GROUPS
    count = len(blocks)
    width = PER_KEY_VALUE * HEAD_SIZE
    first = group * per_group
    in_specs = [
        pl.BlockSpec((responses, length, width), lambda i: (0, 0, first + i)),
        pl.BlockSpec((responses, length, HEAD_SIZE), lambda i: (0, 0, first + i)),
        pl.BlockSpec((responses, length, HEAD_SIZE), lambda i: (0, 0, KEY_VALUE_HEADS + first + i)),
    ]
    for offset in (first, KEY_VALUE_HEADS + first):
        for block in blocks:
            in_specs.append(
                pl.BlockSpec((block.shape[0], HEAD_SIZE), lambda i, offset=offset: (0, offset + i))
            )
    tokens = responses * length
    return pl.pallas_call(
        functools.partial(attention_kernel, count),
        grid=(per_group,),
        in_specs=in_specs,
        out_specs=pl.BlockSpec((tokens, width), lambda i: (0, i)),
        out_shape=jax.ShapeDtypeStruct((tokens, per_group * width), jnp.bfloat16),
        compiler_params=pltpu.CompilerParams(vmem_limit_bytes=60 * 1024 * 1024),
        cost_estimate=pl.CostEstimate(
            flops=2 * 2 * tokens * 2 * per_group * 1152 * 128,
            bytes_accessed=4 * 1024 * 1024,
            transcendentals=2 * tokens * 2 * per_group * 1152,
        ),
    )(queries, response_key_value, response_key_value, *blocks, *blocks)


def project_kernel(sources, weight_ref, gain_ref, *refs):
    out_ref = refs[-1]
    post = gain_ref[0:1, :]
    final = gain_ref[1:2, :]
    part = weight_ref.shape[0] // GROUPS
    for s in range(sources):
        stream_ref, target_ref, *attended = refs[s * (GROUPS + 2) : (s + 1) * (GROUPS + 2)]
        tokens = attended[0].shape[0]
        projected = jnp.dot(
            attended[0][...], weight_ref[0:part, :], preferred_element_type=jnp.float32
        )
        for g in range(1, GROUPS):
            projected += jnp.dot(
                attended[g][...],
                weight_ref[g * part : (g + 1) * part, :],
                preferred_element_type=jnp.float32,
            )
        residual = stream_ref[...].astype(jnp.float32)
        target = target_ref[...].astype(jnp.float32) * final
        scaled = projected * post
        lane = lax.broadcasted_iota(jnp.int32, (tokens, 128), 1)
        packed = jnp.zeros((tokens, 128), jnp.float32)
        terms = (
            projected * projected,
            residual * scaled,
            scaled * scaled,
            target * scaled,
            residual * residual,
            residual * target,
        )
        for k, term in enumerate(terms):
            packed = jnp.where(lane == k, jnp.sum(term, axis=-1, keepdims=True), packed)
        out_ref[s] = jnp.transpose(packed)[0:SUMS, :]


def project(weight, gains, tails, attended):
    sources = len(tails)
    tokens = attended[0][0].shape[0]
    width = weight.shape[1]
    operands = [weight, gains]
    for s in range(sources):
        operands += list(tails[s]) + list(attended[s])
    return pl.pallas_call(
        functools.partial(project_kernel, sources),
        out_shape=jax.ShapeDtypeStruct((sources, SUMS, tokens), jnp.float32),
        compiler_params=pltpu.CompilerParams(vmem_limit_bytes=24 * 1024 * 1024),
        cost_estimate=pl.CostEstimate(
            flops=2 * sources * tokens * 2048 * width,
            bytes_accessed=8 * 1024 * 1024,
            transcendentals=0,
        ),
    )(*operands)


def body(
    queries,
    response_key_value,
    prompt_kv,
    out_weight,
    residual,
    post_gain,
    final_gain,
    target_rows,
    log_norm,
    old_logp,
    ref_logp,
    lengths,
    rewards,
):
    _, responses, length, _ = queries.shape
    tokens = responses * length
    fsdp = lax.axis_size("fsdp")
    dp = lax.axis_size("dp")
    here = lax.axis_index("fsdp")
    columns = D // fsdp

    streams = (residual[0].reshape(tokens, D), target_rows[0].reshape(tokens, D))

    def cut(which, k):
        return lax.dynamic_slice_in_dim(streams[which], (here ^ k) * columns, columns, 1)

    tails = {(0, which): cut(which, 0) for which in (0, 1)}
    far = [(k, which) for k in range(2, fsdp) for which in (0, 1)]
    for which in (0, 1):
        tails[1, which] = swap(cut(which, 1), "fsdp", 1)

    meta = jnp.concatenate([rewards[0], lengths[0].astype(jnp.float32)])
    meta = jnp.pad(meta[None], ((0, 0), (0, length - meta.shape[0])))
    facts = [jnp.concatenate([log_norm[0], old_logp[0], ref_logp[0], meta], axis=0)]
    bit = 1
    while bit < fsdp:
        facts = facts + [swap(value, "fsdp", bit) for value in facts]
        bit *= 2

    def group_sums(facts):
        meta = jnp.stack([value[-1] for value in facts])
        lane = lax.broadcasted_iota(jnp.int32, meta.shape, 1)
        first = jnp.where(lane < responses, meta, 0.0)
        second = jnp.where((lane >= responses) & (lane < 2 * responses), meta, 0.0)
        pair = [jnp.sum(value, axis=1, keepdims=True) for value in (first, second)]
        return jnp.concatenate(pair + [jnp.zeros((meta.shape[0], 126), jnp.float32)], axis=1)

    block = prompt_kv[0]
    gathered = [block]
    rounds = dp // 2
    share = -(-len(far) // rounds)
    rows = block.shape[0]
    crossed = None
    waiting = []
    pieces = {(k, which): cut(which, k) for k, which in far}
    sums = None
    bit = 1
    for step in range(rounds):
        keys = far[step * share : (step + 1) * share]
        for key in keys:
            tails[key] = swap(pieces[key], "fsdp", key[0])
        if sums is not None and bit < dp:
            sums = sums + swap(sums, "dp", bit)
            bit *= 2
        if step == rounds - 1:
            gathered.append(swap(block[: rows // 2], "dp", 1))
            if crossed is None:
                gathered.append(swap(block[rows // 2 :], "dp", 1))
            else:
                gathered.append(around(crossed[rows // 2 :], "dp"))
            waiting = keys
            break
        block, crossed = around(block, "dp"), swap(block, "dp", 1)
        later = far[(step + 1) * share : (step + 2) * share]
        held = [tails[key] for key in keys] + [pieces[key] for key in later]
        held += facts if sums is None else [sums]
        block, crossed, *held = lax.optimization_barrier((block, crossed, *held))
        tails.update(zip(keys, held))
        held = held[len(keys) :]
        pieces.update(zip(later, held))
        held = held[len(later) :]
        if sums is None:
            facts = held
            sums = group_sums(facts)
        else:
            (sums,) = held
        gathered += [block, crossed]
    if sums is None:
        sums = group_sums(facts)
    while bit < dp:
        sums = sums + swap(sums, "dp", bit)
        bit *= 2
    gains = lax.dynamic_slice_in_dim(
        jnp.stack([post_gain, final_gain]), here * columns, columns, 1
    )

    attended = [[None] * GROUPS for _ in range(fsdp)]
    asked = queries[0]
    for g in range(GROUPS):
        attended[0][g] = attend(asked, response_key_value[0], gathered, g)
        last = [tails[key] for key in waiting] + [sums]
        asked, attended[0][g], *last = lax.optimization_barrier((asked, attended[0][g], *last))
        tails.update(zip(waiting, last))
        sums = last[-1]
        if g and fsdp > 2:
            attended[0][g], attended[fsdp // 2][g - 1] = lax.optimization_barrier(
                (attended[0][g], attended[fsdp // 2][g - 1])
            )
        bit = fsdp // 2
        known = [0]
        while bit > 1:
            for k in known:
                attended[k ^ bit][g] = swap(attended[k][g], "fsdp", bit)
            known = known + [k ^ bit for k in known]
            bit //= 2

    facts = jnp.stack(facts)

    def project_some(some):
        for k in some:
            if k & 1:
                attended[k] = [swap(value, "fsdp", 1) for value in attended[k ^ 1]]
        return project(
            out_weight,
            gains,
            [(tails[k, 0], tails[k, 1]) for k in some],
            [attended[k] for k in some],
        )

    near = project_some(list(range(min(2, fsdp))))
    flat = [attended[k][g] for k in range(2, fsdp, 2) for g in range(GROUPS)]
    near, *flat = lax.optimization_barrier((near, *flat))
    for i, k in enumerate(range(2, fsdp, 2)):
        attended[k] = flat[i * GROUPS : (i + 1) * GROUPS]
    parts = [near, project_some(list(range(2, fsdp)))]
    totals = jnp.concatenate(parts, axis=0)
    bit = 1
    while bit < fsdp:
        other = swap(totals, "fsdp", bit)
        totals = totals + jnp.stack([other[k ^ bit] for k in range(fsdp)])
        bit *= 2

    totals = totals.reshape(fsdp, SUMS, responses, length)
    inverse = lax.rsqrt(totals[:, 0] / D + 1e-06)
    square = totals[:, 4] + inverse * (2.0 * totals[:, 1] + inverse * totals[:, 2])
    outer = lax.rsqrt(jnp.maximum(square, 0.0) / D + 1e-06)
    raw = outer * (totals[:, 5] + inverse * totals[:, 3])
    logit = 30.0 * jnp.tanh(raw / 30.0)
    logp = logit - facts[:, 0:responses]
    old = facts[:, responses : 2 * responses]
    ref = facts[:, 2 * responses : 3 * responses]
    meta = facts[:, 3 * responses]
    group_sum, group_count = sums[:, 0], sums[:, 1]
    reward = meta[:, :responses]
    size = meta[:, responses : 2 * responses].astype(jnp.int32)
    position = lax.broadcasted_iota(jnp.int32, (fsdp, responses, length), 2)
    live = position < size[:, :, None]
    log_ratio = jnp.where(live, logp - old, 0.0)
    drift = ref - logp
    kl_terms = jnp.where(live, jnp.exp(drift) - drift - 1.0, 0.0)
    advantage = (reward - (group_sum / (responses * dp))[:, None])[:, :, None]
    ratio = jnp.exp(logp - old)
    surrogate = jnp.minimum(ratio * advantage, jnp.clip(ratio, 0.8, 1.2) * advantage)
    objective = jnp.where(live, 0.04 * kl_terms - surrogate, 0.0)
    loss = jnp.full((1, 128), jnp.sum(objective))
    bit = 1
    while bit < dp:
        loss = loss + swap(loss, "dp", bit)
        bit *= 2
    batch_loss = loss[0, 0] / jnp.sum(group_count)
    return (log_ratio[:1], kl_terms[:1], objective[:1], batch_loss)


def solution(mesh):
    rows4 = P("fsdp", "dp", None, None)
    rows3 = P("fsdp", "dp", None)
    in_specs = (
        rows4,
        rows4,
        rows3,
        P(None, "fsdp"),
        rows4,
        P(),
        P(),
        rows4,
        rows3,
        rows3,
        rows3,
        P("fsdp", "dp"),
        P("fsdp", "dp"),
    )
    out_specs = (rows3, rows3, rows3, P())
    return jax.shard_map(body, mesh=mesh, in_specs=in_specs, out_specs=out_specs, check_vma=False)
```

```python
import functools
import math

import jax
import jax.numpy as jnp
from jax import lax
from jax.experimental import pallas as pl
from jax.experimental.pallas import tpu as pltpu
from jax.sharding import PartitionSpec as P

D = 4608
KEY_VALUE_HEADS = 8
PER_KEY_VALUE = 2
HEAD_SIZE = 128
QPRE = 144
GROUPS = 2
CHUNK = 512
SUMS = 8


def swap(value, axis, bit):
    count = lax.axis_size(axis)
    return lax.ppermute(value, axis, [(i, i ^ bit) for i in range(count)])


def around(value, axis):
    half = lax.axis_size(axis) // 2
    order = list(range(0, half, 2)) + list(range(1, half, 2))[::-1]
    after = {order[i]: order[(i + 1) % half] for i in range(half)}
    return lax.ppermute(
        value, axis, [(i, after[i // 2] * 2 + i % 2) for i in range(2 * half)]
    )


def weigh(q_rows, k_rows):
    scores = lax.dot_general(
        q_rows, k_rows, (((1,), (1,)), ((), ())), preferred_element_type=jnp.float32
    )
    return jnp.exp2(50.0 * math.log2(math.e) * jnp.tanh(scores * (QPRE**-0.5 / 50.0)))


def stacked(q_ref):
    responses, length, _ = q_ref.shape
    q = q_ref[...].reshape(responses * length, PER_KEY_VALUE * HEAD_SIZE)
    return jnp.concatenate(
        [q[:, h * HEAD_SIZE : (h + 1) * HEAD_SIZE] for h in range(PER_KEY_VALUE)], axis=0
    )


def gather_in(stack, key_refs, value_refs, numerator, total):
    keys = jnp.concatenate([ref[...] for ref in key_refs], axis=0)
    values = jnp.concatenate([ref[...] for ref in value_refs], axis=0)
    count = keys.shape[0]
    for start in range(0, count, CHUNK):
        stop = min(start + CHUNK, count)
        weights = weigh(stack, keys[start:stop])
        for lane in range(0, stop - start, HEAD_SIZE):
            piece = weights[:, lane : lane + HEAD_SIZE]
            if piece.shape[1] < HEAD_SIZE:
                piece = jnp.pad(piece, ((0, 0), (0, HEAD_SIZE - piece.shape[1])))
            total = total + piece
        numerator = numerator + jnp.dot(
            weights.astype(jnp.bfloat16), values[start:stop], preferred_element_type=jnp.float32
        )
    return numerator, total


def begin(q_ref, rk_ref, rv_ref, key_refs, value_refs):
    responses, length, _ = q_ref.shape
    later = lax.broadcasted_iota(jnp.int32, (length, length), 0)
    earlier = lax.broadcasted_iota(jnp.int32, (length, length), 1)
    causal = earlier <= later
    stack = stacked(q_ref)
    owned, numerators = [], []
    for i in range(PER_KEY_VALUE * responses):
        r = i % responses
        own = jnp.where(causal, weigh(stack[i * length : (i + 1) * length], rk_ref[r]), 0.0)
        owned.append(own)
        numerators.append(
            jnp.dot(own.astype(jnp.bfloat16), rv_ref[r], preferred_element_type=jnp.float32)
        )
    return gather_in(
        stack,
        key_refs,
        value_refs,
        jnp.concatenate(numerators, axis=0),
        jnp.concatenate(owned, axis=0),
    )


def finish(tokens, numerator, total, out_ref):
    result = (numerator / jnp.sum(total, axis=-1, keepdims=True)).astype(jnp.bfloat16)
    for h in range(PER_KEY_VALUE):
        out_ref[:, h * HEAD_SIZE : (h + 1) * HEAD_SIZE] = result[h * tokens : (h + 1) * tokens]


def first_kernel(count, q_ref, rk_ref, rv_ref, *refs):
    numerator, total = begin(q_ref, rk_ref, rv_ref, refs[:count], refs[count : 2 * count])
    refs[-2][...] = numerator
    refs[-1][...] = total


def whole_kernel(count, q_ref, rk_ref, rv_ref, *refs):
    tokens = q_ref.shape[0] * q_ref.shape[1]
    numerator, total = begin(q_ref, rk_ref, rv_ref, refs[:count], refs[count : 2 * count])
    finish(tokens, numerator, total, refs[-1])


def last_kernel(count, q_ref, numerator_ref, total_ref, *refs):
    key_refs, value_refs, out_ref = refs[:count], refs[count : 2 * count], refs[-1]
    tokens = q_ref.shape[0] * q_ref.shape[1]
    numerator, total = gather_in(
        stacked(q_ref), key_refs, value_refs, numerator_ref[...], total_ref[...]
    )
    finish(tokens, numerator, total, out_ref)


def block_specs(blocks, first):
    return [
        pl.BlockSpec((block.shape[0], HEAD_SIZE), lambda i, offset=offset: (0, offset + i))
        for offset in (first, KEY_VALUE_HEADS + first)
        for block in blocks
    ]


def attention_cost(tokens, heads, positions):
    return pl.CostEstimate(
        flops=2 * 2 * tokens * PER_KEY_VALUE * heads * positions * HEAD_SIZE,
        bytes_accessed=4 * 1024 * 1024,
        transcendentals=2 * tokens * PER_KEY_VALUE * heads * positions,
    )


def attend(queries, response_key_value, state, blocks, group, partial=False):
    responses, length, _ = queries.shape
    per_group = KEY_VALUE_HEADS // GROUPS
    tokens = responses * length
    width = PER_KEY_VALUE * HEAD_SIZE
    first = group * per_group
    in_specs = [pl.BlockSpec((responses, length, width), lambda i: (0, 0, first + i))]
    state_spec = pl.BlockSpec((PER_KEY_VALUE * tokens, HEAD_SIZE), lambda i: (i, 0))
    if state:
        kernel = last_kernel
        operands = state
        in_specs += [state_spec] * 2
    else:
        kernel = first_kernel if partial else whole_kernel
        operands = [response_key_value] * 2
        own = (responses, length, HEAD_SIZE)
        in_specs += [
            pl.BlockSpec(own, lambda i: (0, 0, first + i)),
            pl.BlockSpec(own, lambda i: (0, 0, KEY_VALUE_HEADS + first + i)),
        ]
    if partial:
        out_specs = [state_spec] * 2
        shape = (per_group * PER_KEY_VALUE * tokens, HEAD_SIZE)
        out_shape = [jax.ShapeDtypeStruct(shape, jnp.float32)] * 2
    else:
        out_specs = pl.BlockSpec((tokens, width), lambda i: (0, i))
        out_shape = jax.ShapeDtypeStruct((tokens, per_group * width), jnp.bfloat16)
    return pl.pallas_call(
        functools.partial(kernel, len(blocks)),
        grid=(per_group,),
        in_specs=in_specs + block_specs(blocks, first),
        out_specs=out_specs,
        out_shape=out_shape,
        compiler_params=pltpu.CompilerParams(vmem_limit_bytes=60 * 1024 * 1024),
        cost_estimate=attention_cost(
            tokens, per_group, sum(block.shape[0] for block in blocks) + (0 if state else length)
        ),
    )(queries, *operands, *blocks, *blocks)


def project_kernel(sources, weight_ref, gain_ref, *refs):
    out_ref = refs[-1]
    post = gain_ref[0:1, :]
    final = gain_ref[1:2, :]
    part = weight_ref.shape[0] // GROUPS
    count = GROUPS + 2
    tokens = refs[2].shape[0]
    everything = None
    for g in range(GROUPS):
        rows = jnp.concatenate([refs[s * count + 2 + g][...] for s in range(sources)], axis=0)
        product = jnp.dot(
            rows, weight_ref[g * part : (g + 1) * part, :], preferred_element_type=jnp.float32
        )
        everything = product if g == 0 else everything + product
    for s in range(sources):
        stream_ref, target_ref = refs[s * count : s * count + 2]
        projected = everything[s * tokens : (s + 1) * tokens]
        residual = stream_ref[...].astype(jnp.float32)
        target = target_ref[...].astype(jnp.float32) * final
        scaled = projected * post
        lane = lax.broadcasted_iota(jnp.int32, (tokens, 128), 1)
        packed = jnp.zeros((tokens, 128), jnp.float32)
        terms = (
            projected * projected,
            residual * scaled,
            scaled * scaled,
            target * scaled,
            residual * residual,
            residual * target,
        )
        for k, term in enumerate(terms):
            packed = jnp.where(lane == k, jnp.sum(term, axis=-1, keepdims=True), packed)
        out_ref[s] = jnp.transpose(packed)[0:SUMS, :]


def project(weight, gains, tails, attended):
    sources = len(tails)
    tokens = attended[0][0].shape[0]
    width = weight.shape[1]
    operands = [weight, gains]
    for s in range(sources):
        operands += list(tails[s]) + list(attended[s])
    return pl.pallas_call(
        functools.partial(project_kernel, sources),
        out_shape=jax.ShapeDtypeStruct((sources, SUMS, tokens), jnp.float32),
        compiler_params=pltpu.CompilerParams(vmem_limit_bytes=24 * 1024 * 1024),
        cost_estimate=pl.CostEstimate(
            flops=2 * sources * tokens * 2048 * width,
            bytes_accessed=8 * 1024 * 1024,
            transcendentals=0,
        ),
    )(*operands)


def body(
    queries,
    response_key_value,
    prompt_kv,
    out_weight,
    residual,
    post_gain,
    final_gain,
    target_rows,
    log_norm,
    old_logp,
    ref_logp,
    lengths,
    rewards,
):
    _, responses, length, _ = queries.shape
    tokens = responses * length
    fsdp = lax.axis_size("fsdp")
    dp = lax.axis_size("dp")
    here = lax.axis_index("fsdp")
    columns = D // fsdp

    lane = lax.broadcasted_iota(jnp.int32, (1, length), 1)
    sums = jnp.where(
        lane == 0,
        jnp.sum(rewards[0]),
        jnp.where(lane == 1, jnp.sum(lengths[0]).astype(jnp.float32), 0.0),
    )
    bit = 1

    streams = (residual[0].reshape(tokens, D), target_rows[0].reshape(tokens, D))

    def cut(which, k):
        return lax.dynamic_slice_in_dim(streams[which], (here ^ k) * columns, columns, 1)

    tails = {}
    far = [(k, which) for k in range(2, fsdp) for which in (0, 1)]

    block = prompt_kv[0]
    gathered = [block]
    rounds = dp // 2
    share = -(-len(far) // rounds)
    rows = block.shape[0]
    pieces = {key: cut(key[1], key[0]) for key in far[:share]}
    sums, streams, pieces = lax.optimization_barrier((sums, streams, pieces))
    behind = []
    state = None
    for step in range(rounds):
        keys = far[step * share : (step + 1) * share]
        later = far[(step + 1) * share : (step + 2) * share]
        for key in keys:
            tails[key] = swap(pieces[key], "fsdp", key[0])
        if bit < dp:
            sums = sums + swap(sums, "dp", bit)
            bit *= 2
        if step == rounds - 1:
            final_blocks = [block, crossed]
            final_blocks.append(swap(block[: rows // 2], "dp", 1))
            final_blocks.append(around(crossed[rows // 2 :], "dp"))
            break
        pieces.update({key: cut(key[1], key[0]) for key in later})
        if step == rounds - 2:
            known_blocks = list(gathered)
            state = attend(queries[0], response_key_value[0], None, gathered, 0, True)
        block, crossed = around(block, "dp"), swap(block, "dp", 1)
        held = [tails[key] for key in behind] + [pieces[key] for key in later] + [sums]
        held += state or []
        block, crossed, *held = lax.optimization_barrier((block, crossed, *held))
        if state:
            state = held[-2:]
            held = held[:-2]
        tails.update(zip(behind, held))
        held = held[len(behind) :]
        behind = keys
        pieces.update(zip(later, held))
        sums = held[len(later)]
        gathered += [block, crossed]
        streams, _ = lax.optimization_barrier((streams, sums))
    waiting = far[(rounds - 2) * share :]
    while bit < dp:
        sums = sums + swap(sums, "dp", bit)
        bit *= 2
    for which in (0, 1):
        tails[0, which] = cut(which, 0)
        tails[1, which] = swap(cut(which, 1), "fsdp", 1)

    meta = jnp.concatenate([rewards[0], lengths[0].astype(jnp.float32), sums[0, :2]])
    meta = jnp.pad(meta[None], ((0, 0), (0, length - meta.shape[0])))
    facts = [jnp.concatenate([log_norm[0], old_logp[0], ref_logp[0], meta], axis=0)]
    bit = 1
    while bit < fsdp:
        facts = facts + [swap(value, "fsdp", bit) for value in facts]
        bit *= 2
    gains = lax.dynamic_slice_in_dim(
        jnp.stack([post_gain, final_gain]), here * columns, columns, 1
    )

    attended = [[None] * GROUPS for _ in range(fsdp)]
    asked = queries[0]
    for g in range(GROUPS):
        if g == 0:
            attended[0][g] = attend(asked, response_key_value[0], state, final_blocks, g)
        else:
            attended[0][g] = attend(
                asked, response_key_value[0], None, known_blocks + final_blocks, g
            )
        last = [tails[key] for key in waiting]
        asked, attended[0][g], *last = lax.optimization_barrier((asked, attended[0][g], *last))
        tails.update(zip(waiting, last))
        if g and fsdp > 2:
            attended[0][g], attended[fsdp // 2][g - 1], facts = lax.optimization_barrier(
                (attended[0][g], attended[fsdp // 2][g - 1], facts)
            )
        bit = fsdp // 2
        known = [0]
        while bit > 1:
            for k in known:
                attended[k ^ bit][g] = swap(attended[k][g], "fsdp", bit)
            known = known + [k ^ bit for k in known]
            bit //= 2


    def project_some(some):
        for k in some:
            if k & 1:
                attended[k] = [swap(value, "fsdp", 1) for value in attended[k ^ 1]]
        return project(
            out_weight,
            gains,
            [(tails[k, 0], tails[k, 1]) for k in some],
            [attended[k] for k in some],
        )

    near = project_some(list(range(min(2, fsdp))))
    flat = [attended[k][-1] for k in range(2, fsdp, 2)]
    near, *flat = lax.optimization_barrier((near, *flat))
    for k, value in zip(range(2, fsdp, 2), flat):
        attended[k][-1] = value
    facts = jnp.stack(facts)
    parts = [near, project_some(list(range(2, fsdp)))]
    totals = jnp.concatenate(parts, axis=0)
    bit = 1
    while bit < fsdp:
        other = swap(totals, "fsdp", bit)
        totals = totals + jnp.stack([other[k ^ bit] for k in range(fsdp)])
        bit *= 2

    totals = totals.reshape(fsdp, SUMS, responses, length)
    inverse = lax.rsqrt(totals[:, 0] / D + 1e-06)
    square = totals[:, 4] + inverse * (2.0 * totals[:, 1] + inverse * totals[:, 2])
    outer = lax.rsqrt(jnp.maximum(square, 0.0) / D + 1e-06)
    raw = outer * (totals[:, 5] + inverse * totals[:, 3])
    logit = 30.0 * jnp.tanh(raw / 30.0)
    logp = logit - facts[:, 0:responses]
    old = facts[:, responses : 2 * responses]
    ref = facts[:, 2 * responses : 3 * responses]
    meta = facts[:, 3 * responses]
    group_sum = meta[:, 2 * responses]
    group_count = meta[:, 2 * responses + 1]
    reward = meta[:, :responses]
    size = meta[:, responses : 2 * responses].astype(jnp.int32)
    position = lax.broadcasted_iota(jnp.int32, (fsdp, responses, length), 2)
    live = position < size[:, :, None]
    log_ratio = jnp.where(live, logp - old, 0.0)
    drift = ref - logp
    kl_terms = jnp.where(live, jnp.exp(drift) - drift - 1.0, 0.0)
    advantage = (reward - (group_sum / (responses * dp))[:, None])[:, :, None]
    ratio = jnp.exp(logp - old)
    surrogate = jnp.minimum(ratio * advantage, jnp.clip(ratio, 0.8, 1.2) * advantage)
    objective = jnp.where(live, 0.04 * kl_terms - surrogate, 0.0)
    loss = jnp.full((1, 128), jnp.sum(objective))
    bit = 1
    while bit < dp:
        loss = loss + swap(loss, "dp", bit)
        bit *= 2
    batch_loss = loss[0, 0] / jnp.sum(group_count)
    return (log_ratio[:1], kl_terms[:1], objective[:1], batch_loss)


def solution(mesh):
    rows4 = P("fsdp", "dp", None, None)
    rows3 = P("fsdp", "dp", None)
    in_specs = (
        rows4,
        rows4,
        rows3,
        P(None, "fsdp"),
        rows4,
        P(),
        P(),
        rows4,
        rows3,
        rows3,
        rows3,
        P("fsdp", "dp"),
        P("fsdp", "dp"),
    )
    out_specs = (rows3, rows3, rows3, P())
    return jax.shard_map(body, mesh=mesh, in_specs=in_specs, out_specs=out_specs, check_vma=False)
```

```python
import functools
import math

import jax
import jax.numpy as jnp
from jax import lax
from jax.experimental import pallas as pl
from jax.experimental.pallas import tpu as pltpu
from jax.sharding import PartitionSpec as P

D = 4608
KEY_VALUE_HEADS = 8
PER_KEY_VALUE = 2
HEAD_SIZE = 128
QPRE = 144
GROUPS = 2
CHUNK = 512
SUMS = 8


def swap(value, axis, bit):
    count = lax.axis_size(axis)
    return lax.ppermute(value, axis, [(i, i ^ bit) for i in range(count)])


def around(value, axis):
    half = lax.axis_size(axis) // 2
    order = list(range(0, half, 2)) + list(range(1, half, 2))[::-1]
    after = {order[i]: order[(i + 1) % half] for i in range(half)}
    return lax.ppermute(
        value, axis, [(i, after[i // 2] * 2 + i % 2) for i in range(2 * half)]
    )


def weigh(q_rows, k_rows):
    scores = lax.dot_general(
        q_rows, k_rows, (((1,), (1,)), ((), ())), preferred_element_type=jnp.float32
    )
    return jnp.exp2(50.0 * math.log2(math.e) * jnp.tanh(scores * (QPRE**-0.5 / 50.0)))


def stacked(q_ref):
    responses, length, _ = q_ref.shape
    q = q_ref[...].reshape(responses * length, PER_KEY_VALUE * HEAD_SIZE)
    return jnp.concatenate(
        [q[:, h * HEAD_SIZE : (h + 1) * HEAD_SIZE] for h in range(PER_KEY_VALUE)], axis=0
    )


def gather_in(stack, key_refs, value_refs, numerator, total):
    keys = jnp.concatenate([ref[...] for ref in key_refs], axis=0)
    values = jnp.concatenate([ref[...] for ref in value_refs], axis=0)
    count = keys.shape[0]
    for start in range(0, count, CHUNK):
        stop = min(start + CHUNK, count)
        weights = weigh(stack, keys[start:stop])
        for lane in range(0, stop - start, HEAD_SIZE):
            piece = weights[:, lane : lane + HEAD_SIZE]
            if piece.shape[1] < HEAD_SIZE:
                piece = jnp.pad(piece, ((0, 0), (0, HEAD_SIZE - piece.shape[1])))
            total = total + piece
        numerator = numerator + jnp.dot(
            weights.astype(jnp.bfloat16), values[start:stop], preferred_element_type=jnp.float32
        )
    return numerator, total


def begin(q_ref, rk_ref, rv_ref, key_refs, value_refs):
    responses, length, _ = q_ref.shape
    later = lax.broadcasted_iota(jnp.int32, (length, length), 0)
    earlier = lax.broadcasted_iota(jnp.int32, (length, length), 1)
    causal = earlier <= later
    stack = stacked(q_ref)
    owned, numerators = [], []
    for i in range(PER_KEY_VALUE * responses):
        r = i % responses
        own = jnp.where(causal, weigh(stack[i * length : (i + 1) * length], rk_ref[r]), 0.0)
        owned.append(own)
        numerators.append(
            jnp.dot(own.astype(jnp.bfloat16), rv_ref[r], preferred_element_type=jnp.float32)
        )
    return gather_in(
        stack,
        key_refs,
        value_refs,
        jnp.concatenate(numerators, axis=0),
        jnp.concatenate(owned, axis=0),
    )


def finish(tokens, numerator, total, out_ref):
    result = (numerator / jnp.sum(total, axis=-1, keepdims=True)).astype(jnp.bfloat16)
    for h in range(PER_KEY_VALUE):
        out_ref[:, h * HEAD_SIZE : (h + 1) * HEAD_SIZE] = result[h * tokens : (h + 1) * tokens]


def first_kernel(count, q_ref, rk_ref, rv_ref, *refs):
    numerator, total = begin(q_ref, rk_ref, rv_ref, refs[:count], refs[count : 2 * count])
    refs[-2][...] = numerator
    refs[-1][...] = total


def whole_kernel(count, q_ref, rk_ref, rv_ref, *refs):
    tokens = q_ref.shape[0] * q_ref.shape[1]
    numerator, total = begin(q_ref, rk_ref, rv_ref, refs[:count], refs[count : 2 * count])
    finish(tokens, numerator, total, refs[-1])


def last_kernel(count, q_ref, numerator_ref, total_ref, *refs):
    key_refs, value_refs, out_ref = refs[:count], refs[count : 2 * count], refs[-1]
    tokens = q_ref.shape[0] * q_ref.shape[1]
    numerator, total = gather_in(
        stacked(q_ref), key_refs, value_refs, numerator_ref[...], total_ref[...]
    )
    finish(tokens, numerator, total, out_ref)


def block_specs(blocks, first):
    return [
        pl.BlockSpec((block.shape[0], HEAD_SIZE), lambda i, offset=offset: (0, offset + i))
        for offset in (first, KEY_VALUE_HEADS + first)
        for block in blocks
    ]


def attention_cost(tokens, heads, positions):
    return pl.CostEstimate(
        flops=2 * 2 * tokens * PER_KEY_VALUE * heads * positions * HEAD_SIZE,
        bytes_accessed=4 * 1024 * 1024,
        transcendentals=2 * tokens * PER_KEY_VALUE * heads * positions,
    )


def attend(queries, response_key_value, state, blocks, group, partial=False):
    responses, length, _ = queries.shape
    per_group = KEY_VALUE_HEADS // GROUPS
    tokens = responses * length
    width = PER_KEY_VALUE * HEAD_SIZE
    first = group * per_group
    in_specs = [pl.BlockSpec((responses, length, width), lambda i: (0, 0, first + i))]
    state_spec = pl.BlockSpec((PER_KEY_VALUE * tokens, HEAD_SIZE), lambda i: (i, 0))
    if state:
        kernel = last_kernel
        operands = state
        in_specs += [state_spec] * 2
    else:
        kernel = first_kernel if partial else whole_kernel
        operands = [response_key_value] * 2
        own = (responses, length, HEAD_SIZE)
        in_specs += [
            pl.BlockSpec(own, lambda i: (0, 0, first + i)),
            pl.BlockSpec(own, lambda i: (0, 0, KEY_VALUE_HEADS + first + i)),
        ]
    if partial:
        out_specs = [state_spec] * 2
        shape = (per_group * PER_KEY_VALUE * tokens, HEAD_SIZE)
        out_shape = [jax.ShapeDtypeStruct(shape, jnp.float32)] * 2
    else:
        out_specs = pl.BlockSpec((tokens, width), lambda i: (0, i))
        out_shape = jax.ShapeDtypeStruct((tokens, per_group * width), jnp.bfloat16)
    return pl.pallas_call(
        functools.partial(kernel, len(blocks)),
        grid=(per_group,),
        in_specs=in_specs + block_specs(blocks, first),
        out_specs=out_specs,
        out_shape=out_shape,
        compiler_params=pltpu.CompilerParams(vmem_limit_bytes=60 * 1024 * 1024),
        cost_estimate=attention_cost(
            tokens, per_group, sum(block.shape[0] for block in blocks) + (0 if state else length)
        ),
    )(queries, *operands, *blocks, *blocks)


def project_kernel(sources, weight_ref, gain_ref, *refs):
    out_ref = refs[-1]
    post = gain_ref[0:1, :]
    final = gain_ref[1:2, :]
    part = weight_ref.shape[0] // GROUPS
    count = GROUPS + 1
    tokens = refs[1].shape[0]
    everything = None
    for g in range(GROUPS):
        rows = jnp.concatenate([refs[s * count + 1 + g][...] for s in range(sources)], axis=0)
        product = jnp.dot(
            rows, weight_ref[g * part : (g + 1) * part, :], preferred_element_type=jnp.float32
        )
        everything = product if g == 0 else everything + product
    for s in range(sources):
        tail_ref = refs[s * count]
        projected = everything[s * tokens : (s + 1) * tokens]
        residual = tail_ref[0:tokens, :].astype(jnp.float32)
        target = tail_ref[tokens : 2 * tokens, :].astype(jnp.float32) * final
        scaled = projected * post
        lane = lax.broadcasted_iota(jnp.int32, (tokens, 128), 1)
        packed = jnp.zeros((tokens, 128), jnp.float32)
        terms = (
            projected * projected,
            residual * scaled,
            scaled * scaled,
            target * scaled,
            residual * residual,
            residual * target,
        )
        for k, term in enumerate(terms):
            packed = jnp.where(lane == k, jnp.sum(term, axis=-1, keepdims=True), packed)
        out_ref[s] = jnp.transpose(packed)[0:SUMS, :]


def project(weight, gains, tails, attended, limit):
    sources = len(tails)
    tokens = attended[0][0].shape[0]
    width = weight.shape[1]
    operands = [weight, gains]
    for s in range(sources):
        operands += [tails[s]] + list(attended[s])
    return pl.pallas_call(
        functools.partial(project_kernel, sources),
        out_shape=jax.ShapeDtypeStruct((sources, SUMS, tokens), jnp.float32),
        compiler_params=pltpu.CompilerParams(vmem_limit_bytes=limit * 1024 * 1024),
        cost_estimate=pl.CostEstimate(
            flops=2 * sources * tokens * 2048 * width,
            bytes_accessed=8 * 1024 * 1024,
            transcendentals=0,
        ),
    )(*operands)


def body(
    queries,
    response_key_value,
    prompt_kv,
    out_weight,
    residual,
    post_gain,
    final_gain,
    target_rows,
    log_norm,
    old_logp,
    ref_logp,
    lengths,
    rewards,
):
    _, responses, length, _ = queries.shape
    tokens = responses * length
    fsdp = lax.axis_size("fsdp")
    dp = lax.axis_size("dp")
    here = lax.axis_index("fsdp")
    columns = D // fsdp

    lane = lax.broadcasted_iota(jnp.int32, (1, length), 1)
    sums = jnp.where(
        lane == 0,
        jnp.sum(rewards[0]),
        jnp.where(lane == 1, jnp.sum(lengths[0]).astype(jnp.float32), 0.0),
    )
    bit = 1

    streams = (residual[0].reshape(tokens, D), target_rows[0].reshape(tokens, D))

    def cut(k):
        start = (here ^ k) * columns
        return jnp.concatenate(
            [lax.dynamic_slice_in_dim(value, start, columns, 1) for value in streams], axis=0
        )

    tails = {}
    far = list(range(2, fsdp))

    block = prompt_kv[0]
    gathered = [block]
    rounds = dp // 2
    share = -(-len(far) // max(rounds - 2, 1))
    rows = block.shape[0]
    pieces = {key: cut(key) for key in far[:share]}
    state = None
    for step in range(rounds):
        keys = far[step * share : (step + 1) * share]
        later = far[(step + 1) * share : (step + 2) * share]
        for key in keys:
            tails[key] = swap(pieces[key], "fsdp", key)
        if step and bit < dp:
            sums = sums + swap(sums, "dp", bit)
            bit *= 2
        if step == rounds - 1:
            final_blocks = [block, crossed]
            final_blocks.append(swap(block[: rows // 2], "dp", 1))
            final_blocks.append(around(crossed[rows // 2 :], "dp"))
            break
        pieces.update({key: cut(key) for key in later})
        if step == rounds - 2:
            known_blocks = list(gathered)
            state = attend(queries[0], response_key_value[0], None, gathered, 0, True)
        block, crossed = around(block, "dp"), swap(block, "dp", 1)
        behind = far[max(step - 2, 0) * share : max(step - 1, 0) * share]
        held = [tails[key] for key in behind] + [pieces[key] for key in later] + [sums]
        held += state or []
        block, crossed, *held = lax.optimization_barrier((block, crossed, *held))
        if state:
            state = held[-2:]
            held = held[:-2]
        tails.update(zip(behind, held))
        held = held[len(behind) :]
        pieces.update(zip(later, held))
        sums = held[len(later)]
        gathered += [block, crossed]
        streams, _ = lax.optimization_barrier((streams, sums))
    waiting = far[(rounds - 3) * share :]
    while bit < dp:
        sums = sums + swap(sums, "dp", bit)
        bit *= 2
    tails[0] = cut(0)
    tails[1] = swap(cut(1), "fsdp", 1)

    meta = jnp.concatenate([rewards[0], lengths[0].astype(jnp.float32), sums[0, :2]])
    meta = jnp.pad(meta[None], ((0, 0), (0, length - meta.shape[0])))
    facts = [jnp.concatenate([log_norm[0], old_logp[0], ref_logp[0], meta], axis=0)]
    bit = 1
    while bit < fsdp:
        facts = facts + [swap(value, "fsdp", bit) for value in facts]
        bit *= 2
    gains = lax.dynamic_slice_in_dim(
        jnp.stack([post_gain, final_gain]), here * columns, columns, 1
    )

    attended = [[None] * GROUPS for _ in range(fsdp)]
    asked = queries[0]
    for g in range(GROUPS):
        if g == 0:
            attended[0][g] = attend(asked, response_key_value[0], state, final_blocks, g)
        else:
            attended[0][g] = attend(
                asked, response_key_value[0], None, known_blocks + final_blocks, g
            )
        last = [tails[key] for key in waiting]
        asked, attended[0][g], *last = lax.optimization_barrier((asked, attended[0][g], *last))
        tails.update(zip(waiting, last))
        if g and fsdp > 2:
            attended[0][g], attended[fsdp // 2][g - 1] = lax.optimization_barrier(
                (attended[0][g], attended[fsdp // 2][g - 1])
            )
        bit = fsdp // 2
        known = [0]
        while bit > 1:
            for k in known:
                attended[k ^ bit][g] = swap(attended[k][g], "fsdp", bit)
            known = known + [k ^ bit for k in known]
            bit //= 2


    def project_some(some, limit):
        for k in some:
            if k & 1:
                attended[k] = [swap(value, "fsdp", 1) for value in attended[k ^ 1]]
        return project(
            out_weight,
            gains,
            [tails[k] for k in some],
            [attended[k] for k in some],
            limit,
        )

    near = project_some(list(range(min(2, fsdp))), 24)
    flat = [attended[k][-1] for k in range(2, fsdp, 2)]
    near, facts, *flat = lax.optimization_barrier((near, facts, *flat))
    for k, value in zip(range(2, fsdp, 2), flat):
        attended[k][-1] = value
    facts = jnp.stack(facts)
    parts = [near, project_some(list(range(2, fsdp)), min(6 * (fsdp - 2), 60))]
    totals = jnp.concatenate(parts, axis=0)
    bit = 1
    while bit < fsdp:
        other = swap(totals, "fsdp", bit)
        totals = totals + jnp.stack([other[k ^ bit] for k in range(fsdp)])
        bit *= 2

    totals = totals.reshape(fsdp, SUMS, responses, length)
    inverse = lax.rsqrt(totals[:, 0] / D + 1e-06)
    square = totals[:, 4] + inverse * (2.0 * totals[:, 1] + inverse * totals[:, 2])
    outer = lax.rsqrt(jnp.maximum(square, 0.0) / D + 1e-06)
    raw = outer * (totals[:, 5] + inverse * totals[:, 3])
    logit = 30.0 * jnp.tanh(raw / 30.0)
    logp = logit - facts[:, 0:responses]
    old = facts[:, responses : 2 * responses]
    ref = facts[:, 2 * responses : 3 * responses]
    meta = facts[:, 3 * responses]
    group_sum = meta[:, 2 * responses]
    group_count = meta[:, 2 * responses + 1]
    reward = meta[:, :responses]
    size = meta[:, responses : 2 * responses].astype(jnp.int32)
    position = lax.broadcasted_iota(jnp.int32, (fsdp, responses, length), 2)
    live = position < size[:, :, None]
    log_ratio = jnp.where(live, logp - old, 0.0)
    drift = ref - logp
    kl_terms = jnp.where(live, jnp.exp(drift) - drift - 1.0, 0.0)
    advantage = (reward - (group_sum / (responses * dp))[:, None])[:, :, None]
    ratio = jnp.exp(logp - old)
    surrogate = jnp.minimum(ratio * advantage, jnp.clip(ratio, 0.8, 1.2) * advantage)
    objective = jnp.where(live, 0.04 * kl_terms - surrogate, 0.0)
    loss = jnp.full((1, 128), jnp.sum(objective))
    bit = 1
    while bit < dp:
        loss = loss + swap(loss, "dp", bit)
        bit *= 2
    batch_loss = loss[0, 0] / jnp.sum(group_count)
    return (log_ratio[:1], kl_terms[:1], objective[:1], batch_loss)


def solution(mesh):
    rows4 = P("fsdp", "dp", None, None)
    rows3 = P("fsdp", "dp", None)
    in_specs = (
        rows4,
        rows4,
        rows3,
        P(None, "fsdp"),
        rows4,
        P(),
        P(),
        rows4,
        rows3,
        rows3,
        rows3,
        P("fsdp", "dp"),
        P("fsdp", "dp"),
    )
    out_specs = (rows3, rows3, rows3, P())
    return jax.shard_map(body, mesh=mesh, in_specs=in_specs, out_specs=out_specs, check_vma=False)
```

```python
import functools
import math

import jax
import jax.numpy as jnp
from jax import lax
from jax.experimental import pallas as pl
from jax.experimental.pallas import tpu as pltpu
from jax.sharding import PartitionSpec as P

D = 4608
KEY_VALUE_HEADS = 8
PER_KEY_VALUE = 2
HEAD_SIZE = 128
QPRE = 144
GROUPS = 2
CHUNK = 512
SUMS = 8


def swap(value, axis, bit):
    count = lax.axis_size(axis)
    return lax.ppermute(value, axis, [(i, i ^ bit) for i in range(count)])


def around(value, axis):
    half = lax.axis_size(axis) // 2
    order = list(range(0, half, 2)) + list(range(1, half, 2))[::-1]
    after = {order[i]: order[(i + 1) % half] for i in range(half)}
    return lax.ppermute(
        value, axis, [(i, after[i // 2] * 2 + i % 2) for i in range(2 * half)]
    )


def weigh(q_rows, k_rows):
    scores = lax.dot_general(
        q_rows, k_rows, (((1,), (1,)), ((), ())), preferred_element_type=jnp.float32
    )
    return jnp.exp2(50.0 * math.log2(math.e) * jnp.tanh(scores * (QPRE**-0.5 / 50.0)))


def stacked(q_ref):
    responses, length, _ = q_ref.shape
    q = q_ref[...].reshape(responses * length, PER_KEY_VALUE * HEAD_SIZE)
    return jnp.concatenate(
        [q[:, h * HEAD_SIZE : (h + 1) * HEAD_SIZE] for h in range(PER_KEY_VALUE)], axis=0
    )


def gather_in(stack, key_refs, value_refs, numerator, total):
    keys = jnp.concatenate([ref[...] for ref in key_refs], axis=0)
    values = jnp.concatenate([ref[...] for ref in value_refs], axis=0)
    count = keys.shape[0]
    for start in range(0, count, CHUNK):
        stop = min(start + CHUNK, count)
        weights = weigh(stack, keys[start:stop])
        for lane in range(0, stop - start, HEAD_SIZE):
            piece = weights[:, lane : lane + HEAD_SIZE]
            if piece.shape[1] < HEAD_SIZE:
                piece = jnp.pad(piece, ((0, 0), (0, HEAD_SIZE - piece.shape[1])))
            total = total + piece
        numerator = numerator + jnp.dot(
            weights.astype(jnp.bfloat16), values[start:stop], preferred_element_type=jnp.float32
        )
    return numerator, total


def begin(q_ref, rk_ref, rv_ref, key_refs, value_refs):
    responses, length, _ = q_ref.shape
    later = lax.broadcasted_iota(jnp.int32, (length, length), 0)
    earlier = lax.broadcasted_iota(jnp.int32, (length, length), 1)
    causal = earlier <= later
    stack = stacked(q_ref)
    owned, numerators = [], []
    for i in range(PER_KEY_VALUE * responses):
        r = i % responses
        own = jnp.where(causal, weigh(stack[i * length : (i + 1) * length], rk_ref[r]), 0.0)
        owned.append(own)
        numerators.append(
            jnp.dot(own.astype(jnp.bfloat16), rv_ref[r], preferred_element_type=jnp.float32)
        )
    return gather_in(
        stack,
        key_refs,
        value_refs,
        jnp.concatenate(numerators, axis=0),
        jnp.concatenate(owned, axis=0),
    )


def finish(tokens, numerator, total, out_ref):
    result = (numerator / jnp.sum(total, axis=-1, keepdims=True)).astype(jnp.bfloat16)
    for h in range(PER_KEY_VALUE):
        out_ref[:, h * HEAD_SIZE : (h + 1) * HEAD_SIZE] = result[h * tokens : (h + 1) * tokens]


def first_kernel(count, q_ref, rk_ref, rv_ref, *refs):
    numerator, total = begin(q_ref, rk_ref, rv_ref, refs[:count], refs[count : 2 * count])
    refs[-2][...] = numerator
    refs[-1][...] = total


def whole_kernel(count, q_ref, rk_ref, rv_ref, *refs):
    tokens = q_ref.shape[0] * q_ref.shape[1]
    numerator, total = begin(q_ref, rk_ref, rv_ref, refs[:count], refs[count : 2 * count])
    finish(tokens, numerator, total, refs[-1])


def last_kernel(count, q_ref, numerator_ref, total_ref, *refs):
    key_refs, value_refs, out_ref = refs[:count], refs[count : 2 * count], refs[-1]
    tokens = q_ref.shape[0] * q_ref.shape[1]
    numerator, total = gather_in(
        stacked(q_ref), key_refs, value_refs, numerator_ref[...], total_ref[...]
    )
    finish(tokens, numerator, total, out_ref)


def block_specs(blocks, first):
    return [
        pl.BlockSpec((block.shape[0], HEAD_SIZE), lambda i, offset=offset: (0, offset + i))
        for offset in (first, KEY_VALUE_HEADS + first)
        for block in blocks
    ]


def attention_cost(tokens, heads, positions):
    return pl.CostEstimate(
        flops=2 * 2 * tokens * PER_KEY_VALUE * heads * positions * HEAD_SIZE,
        bytes_accessed=4 * 1024 * 1024,
        transcendentals=2 * tokens * PER_KEY_VALUE * heads * positions,
    )


def attend(queries, response_key_value, state, blocks, group, partial=False):
    responses, length, _ = queries.shape
    per_group = KEY_VALUE_HEADS // GROUPS
    tokens = responses * length
    width = PER_KEY_VALUE * HEAD_SIZE
    first = group * per_group
    in_specs = [pl.BlockSpec((responses, length, width), lambda i: (0, 0, first + i))]
    state_spec = pl.BlockSpec((PER_KEY_VALUE * tokens, HEAD_SIZE), lambda i: (i, 0))
    if state:
        kernel = last_kernel
        operands = state
        in_specs += [state_spec] * 2
    else:
        kernel = first_kernel if partial else whole_kernel
        operands = [response_key_value] * 2
        own = (responses, length, HEAD_SIZE)
        in_specs += [
            pl.BlockSpec(own, lambda i: (0, 0, first + i)),
            pl.BlockSpec(own, lambda i: (0, 0, KEY_VALUE_HEADS + first + i)),
        ]
    if partial:
        out_specs = [state_spec] * 2
        shape = (per_group * PER_KEY_VALUE * tokens, HEAD_SIZE)
        out_shape = [jax.ShapeDtypeStruct(shape, jnp.float32)] * 2
    else:
        out_specs = pl.BlockSpec((tokens, width), lambda i: (0, i))
        out_shape = jax.ShapeDtypeStruct((tokens, per_group * width), jnp.bfloat16)
    return pl.pallas_call(
        functools.partial(kernel, len(blocks)),
        grid=(per_group,),
        in_specs=in_specs + block_specs(blocks, first),
        out_specs=out_specs,
        out_shape=out_shape,
        compiler_params=pltpu.CompilerParams(vmem_limit_bytes=60 * 1024 * 1024),
        cost_estimate=attention_cost(
            tokens, per_group, sum(block.shape[0] for block in blocks) + (0 if state else length)
        ),
    )(queries, *operands, *blocks, *blocks)


def project_kernel(sources, weight_ref, gain_ref, *refs):
    out_ref = refs[-1]
    post = gain_ref[0:1, :]
    final = gain_ref[1:2, :]
    part = weight_ref.shape[0] // GROUPS
    count = GROUPS + 1
    tokens = refs[1].shape[0]
    everything = None
    for g in range(GROUPS):
        rows = jnp.concatenate([refs[s * count + 1 + g][...] for s in range(sources)], axis=0)
        product = jnp.dot(
            rows, weight_ref[g * part : (g + 1) * part, :], preferred_element_type=jnp.float32
        )
        everything = product if g == 0 else everything + product
    for s in range(sources):
        tail_ref = refs[s * count]
        projected = everything[s * tokens : (s + 1) * tokens]
        residual = tail_ref[0:tokens, :].astype(jnp.float32)
        target = tail_ref[tokens : 2 * tokens, :].astype(jnp.float32) * final
        scaled = projected * post
        lane = lax.broadcasted_iota(jnp.int32, (tokens, 128), 1)
        packed = jnp.zeros((tokens, 128), jnp.float32)
        terms = (
            projected * projected,
            residual * scaled,
            scaled * scaled,
            target * scaled,
            residual * residual,
            residual * target,
        )
        for k, term in enumerate(terms):
            packed = jnp.where(lane == k, jnp.sum(term, axis=-1, keepdims=True), packed)
        out_ref[s] = jnp.transpose(packed)[0:SUMS, :]


def project(weight, gains, tails, attended, limit):
    sources = len(tails)
    tokens = attended[0][0].shape[0]
    width = weight.shape[1]
    operands = [weight, gains]
    for s in range(sources):
        operands += [tails[s]] + list(attended[s])
    return pl.pallas_call(
        functools.partial(project_kernel, sources),
        out_shape=jax.ShapeDtypeStruct((sources, SUMS, tokens), jnp.float32),
        compiler_params=pltpu.CompilerParams(vmem_limit_bytes=limit * 1024 * 1024),
        cost_estimate=pl.CostEstimate(
            flops=2 * sources * tokens * 2048 * width,
            bytes_accessed=8 * 1024 * 1024,
            transcendentals=0,
        ),
    )(*operands)


def body(
    queries,
    response_key_value,
    prompt_kv,
    out_weight,
    residual,
    post_gain,
    final_gain,
    target_rows,
    log_norm,
    old_logp,
    ref_logp,
    lengths,
    rewards,
):
    _, responses, length, _ = queries.shape
    tokens = responses * length
    fsdp = lax.axis_size("fsdp")
    dp = lax.axis_size("dp")
    here = lax.axis_index("fsdp")
    columns = D // fsdp

    lane = lax.broadcasted_iota(jnp.int32, (1, length), 1)
    sums = jnp.where(
        lane == 0,
        jnp.sum(rewards[0]),
        jnp.where(lane == 1, jnp.sum(lengths[0]).astype(jnp.float32), 0.0),
    )
    bit = 1

    streams = (residual[0].reshape(tokens, D), target_rows[0].reshape(tokens, D))

    def cut(k):
        start = (here ^ k) * columns
        return jnp.concatenate(
            [lax.dynamic_slice_in_dim(value, start, columns, 1) for value in streams], axis=0
        )

    tails = {}
    far = list(range(2, fsdp))

    block = prompt_kv[0]
    gathered = [block]
    rounds = dp // 2
    share = -(-len(far) // max(rounds - 2, 1))
    rows = block.shape[0]
    pieces = {key: cut(key) for key in far[:share]}
    state = None
    for step in range(rounds):
        keys = far[step * share : (step + 1) * share]
        later = far[(step + 1) * share : (step + 2) * share]
        for key in keys:
            tails[key] = swap(pieces[key], "fsdp", key)
        if step and bit < dp:
            sums = sums + swap(sums, "dp", bit)
            bit *= 2
        if step == rounds - 1:
            final_blocks = [block, crossed]
            final_blocks.append(swap(block[: rows // 2], "dp", 1))
            final_blocks.append(around(crossed[rows // 2 :], "dp"))
            sums, state = lax.optimization_barrier((sums, state))
            break
        pieces.update({key: cut(key) for key in later})
        if step == rounds - 2:
            known_blocks = list(gathered)
            state = attend(queries[0], response_key_value[0], None, gathered, 0, True)
        block, crossed = around(block, "dp"), swap(block, "dp", 1)
        behind = far[max(step - 2, 0) * share : max(step - 1, 0) * share]
        held = [tails[key] for key in behind] + [pieces[key] for key in later] + [sums]
        held += state or []
        block, crossed, *held = lax.optimization_barrier((block, crossed, *held))
        if state:
            state = held[-2:]
            held = held[:-2]
        tails.update(zip(behind, held))
        held = held[len(behind) :]
        pieces.update(zip(later, held))
        sums = held[len(later)]
        gathered += [block, crossed]
        streams, _ = lax.optimization_barrier((streams, sums))
    waiting = far[(rounds - 3) * share :]
    while bit < dp:
        sums = sums + swap(sums, "dp", bit)
        bit *= 2
    tails[0] = cut(0)
    tails[1] = swap(cut(1), "fsdp", 1)

    meta = jnp.concatenate([rewards[0], lengths[0].astype(jnp.float32), sums[0, :2]])
    meta = jnp.pad(meta[None], ((0, 0), (0, length - meta.shape[0])))
    facts = [jnp.concatenate([log_norm[0], old_logp[0], ref_logp[0], meta], axis=0)]
    bit = 1
    while bit < fsdp:
        facts = facts + [swap(value, "fsdp", bit) for value in facts]
        bit *= 2
    gains = lax.dynamic_slice_in_dim(
        jnp.stack([post_gain, final_gain]), here * columns, columns, 1
    )

    attended = [[None] * GROUPS for _ in range(fsdp)]
    asked = queries[0]
    for g in range(GROUPS):
        if g == 0:
            attended[0][g] = attend(asked, response_key_value[0], state, final_blocks, g)
        else:
            attended[0][g] = attend(
                asked, response_key_value[0], None, known_blocks + final_blocks, g
            )
        last = [tails[key] for key in waiting]
        asked, attended[0][g], *last = lax.optimization_barrier((asked, attended[0][g], *last))
        tails.update(zip(waiting, last))
        if g and fsdp > 2:
            attended[0][g], attended[fsdp // 2][g - 1] = lax.optimization_barrier(
                (attended[0][g], attended[fsdp // 2][g - 1])
            )
        bit = fsdp // 2
        known = [0]
        while bit > 1:
            for k in known:
                attended[k ^ bit][g] = swap(attended[k][g], "fsdp", bit)
            known = known + [k ^ bit for k in known]
            bit //= 2


    def project_some(some, limit):
        for k in some:
            if k & 1:
                attended[k] = [swap(value, "fsdp", 1) for value in attended[k ^ 1]]
        return project(
            out_weight,
            gains,
            [tails[k] for k in some],
            [attended[k] for k in some],
            limit,
        )

    near = project_some(list(range(min(2, fsdp))), 24)
    flat = [attended[k][-1] for k in range(2, fsdp, 2)]
    near, facts, *flat = lax.optimization_barrier((near, facts, *flat))
    for k, value in zip(range(2, fsdp, 2), flat):
        attended[k][-1] = value
    facts = jnp.stack(facts)
    parts = [near, project_some(list(range(2, fsdp)), min(6 * (fsdp - 2), 60))]
    totals = jnp.concatenate(parts, axis=0)
    bit = 1
    while bit < fsdp:
        other = swap(totals, "fsdp", bit)
        totals = totals + jnp.stack([other[k ^ bit] for k in range(fsdp)])
        bit *= 2

    totals = totals.reshape(fsdp, SUMS, responses, length)
    inverse = lax.rsqrt(totals[:, 0] / D + 1e-06)
    square = totals[:, 4] + inverse * (2.0 * totals[:, 1] + inverse * totals[:, 2])
    outer = lax.rsqrt(jnp.maximum(square, 0.0) / D + 1e-06)
    raw = outer * (totals[:, 5] + inverse * totals[:, 3])
    logit = 30.0 * jnp.tanh(raw / 30.0)
    logp = logit - facts[:, 0:responses]
    old = facts[:, responses : 2 * responses]
    ref = facts[:, 2 * responses : 3 * responses]
    meta = facts[:, 3 * responses]
    group_sum = meta[:, 2 * responses]
    group_count = meta[:, 2 * responses + 1]
    reward = meta[:, :responses]
    size = meta[:, responses : 2 * responses].astype(jnp.int32)
    position = lax.broadcasted_iota(jnp.int32, (fsdp, responses, length), 2)
    live = position < size[:, :, None]
    log_ratio = jnp.where(live, logp - old, 0.0)
    drift = ref - logp
    kl_terms = jnp.where(live, jnp.exp(drift) - drift - 1.0, 0.0)
    advantage = (reward - (group_sum / (responses * dp))[:, None])[:, :, None]
    ratio = jnp.exp(logp - old)
    surrogate = jnp.minimum(ratio * advantage, jnp.clip(ratio, 0.8, 1.2) * advantage)
    objective = jnp.where(live, 0.04 * kl_terms - surrogate, 0.0)
    loss = jnp.sum(objective, axis=(0, 1))[None]
    bit = 1
    while bit < dp:
        loss = loss + swap(loss, "dp", bit)
        bit *= 2
    batch_loss = jnp.sum(loss) / jnp.sum(group_count)
    return (log_ratio[:1], kl_terms[:1], objective[:1], batch_loss)


def solution(mesh):
    rows4 = P("fsdp", "dp", None, None)
    rows3 = P("fsdp", "dp", None)
    in_specs = (
        rows4,
        rows4,
        rows3,
        P(None, "fsdp"),
        rows4,
        P(),
        P(),
        rows4,
        rows3,
        rows3,
        rows3,
        P("fsdp", "dp"),
        P("fsdp", "dp"),
    )
    out_specs = (rows3, rows3, rows3, P())
    return jax.shard_map(body, mesh=mesh, in_specs=in_specs, out_specs=out_specs, check_vma=False)
```

```python
import functools
import math

import jax
import jax.numpy as jnp
from jax import lax
from jax.experimental import pallas as pl
from jax.experimental.pallas import tpu as pltpu
from jax.sharding import PartitionSpec as P

D = 4608
KEY_VALUE_HEADS = 8
PER_KEY_VALUE = 2
HEAD_SIZE = 128
QPRE = 144
GROUPS = 2
CHUNK = 512
SUMS = 8


def swap(value, axis, bit):
    count = lax.axis_size(axis)
    return lax.ppermute(value, axis, [(i, i ^ bit) for i in range(count)])


def around(value, axis):
    half = lax.axis_size(axis) // 2
    order = list(range(0, half, 2)) + list(range(1, half, 2))[::-1]
    after = {order[i]: order[(i + 1) % half] for i in range(half)}
    return lax.ppermute(
        value, axis, [(i, after[i // 2] * 2 + i % 2) for i in range(2 * half)]
    )


def weigh(q_rows, k_rows):
    scores = lax.dot_general(
        q_rows, k_rows, (((1,), (1,)), ((), ())), preferred_element_type=jnp.float32
    )
    return jnp.exp2(50.0 * math.log2(math.e) * jnp.tanh(scores * (QPRE**-0.5 / 50.0)))


def stacked(q_ref):
    responses, length, _ = q_ref.shape
    q = q_ref[...].reshape(responses * length, PER_KEY_VALUE * HEAD_SIZE)
    return jnp.concatenate(
        [q[:, h * HEAD_SIZE : (h + 1) * HEAD_SIZE] for h in range(PER_KEY_VALUE)], axis=0
    )


def gather_in(stack, key_refs, value_refs, numerator, total):
    keys = jnp.concatenate([ref[...] for ref in key_refs], axis=0)
    values = jnp.concatenate([ref[...] for ref in value_refs], axis=0)
    count = keys.shape[0]
    for start in range(0, count, CHUNK):
        stop = min(start + CHUNK, count)
        weights = weigh(stack, keys[start:stop])
        for lane in range(0, stop - start, HEAD_SIZE):
            piece = weights[:, lane : lane + HEAD_SIZE]
            if piece.shape[1] < HEAD_SIZE:
                piece = jnp.pad(piece, ((0, 0), (0, HEAD_SIZE - piece.shape[1])))
            total = total + piece
        numerator = numerator + jnp.dot(
            weights.astype(jnp.bfloat16), values[start:stop], preferred_element_type=jnp.float32
        )
    return numerator, total


def begin(q_ref, rk_ref, rv_ref, key_refs, value_refs):
    responses, length, _ = q_ref.shape
    later = lax.broadcasted_iota(jnp.int32, (length, length), 0)
    earlier = lax.broadcasted_iota(jnp.int32, (length, length), 1)
    causal = earlier <= later
    stack = stacked(q_ref)
    owned, numerators = [], []
    for i in range(PER_KEY_VALUE * responses):
        r = i % responses
        own = jnp.where(causal, weigh(stack[i * length : (i + 1) * length], rk_ref[r]), 0.0)
        owned.append(own)
        numerators.append(
            jnp.dot(own.astype(jnp.bfloat16), rv_ref[r], preferred_element_type=jnp.float32)
        )
    return gather_in(
        stack,
        key_refs,
        value_refs,
        jnp.concatenate(numerators, axis=0),
        jnp.concatenate(owned, axis=0),
    )


def finish(tokens, numerator, total, out_ref):
    result = (numerator / jnp.sum(total, axis=-1, keepdims=True)).astype(jnp.bfloat16)
    for h in range(PER_KEY_VALUE):
        out_ref[:, h * HEAD_SIZE : (h + 1) * HEAD_SIZE] = result[h * tokens : (h + 1) * tokens]


def first_kernel(count, q_ref, rk_ref, rv_ref, *refs):
    numerator, total = begin(q_ref, rk_ref, rv_ref, refs[:count], refs[count : 2 * count])
    refs[-2][...] = numerator
    refs[-1][...] = total


def whole_kernel(count, q_ref, rk_ref, rv_ref, *refs):
    tokens = q_ref.shape[0] * q_ref.shape[1]
    numerator, total = begin(q_ref, rk_ref, rv_ref, refs[:count], refs[count : 2 * count])
    finish(tokens, numerator, total, refs[-1])


def last_kernel(count, q_ref, numerator_ref, total_ref, *refs):
    key_refs, value_refs, out_ref = refs[:count], refs[count : 2 * count], refs[-1]
    tokens = q_ref.shape[0] * q_ref.shape[1]
    numerator, total = gather_in(
        stacked(q_ref), key_refs, value_refs, numerator_ref[...], total_ref[...]
    )
    finish(tokens, numerator, total, out_ref)


def block_specs(blocks, first):
    return [
        pl.BlockSpec((block.shape[0], HEAD_SIZE), lambda i, offset=offset: (0, offset + i))
        for offset in (first, KEY_VALUE_HEADS + first)
        for block in blocks
    ]


def attention_cost(tokens, heads, positions):
    return pl.CostEstimate(
        flops=2 * 2 * tokens * PER_KEY_VALUE * heads * positions * HEAD_SIZE,
        bytes_accessed=4 * 1024 * 1024,
        transcendentals=2 * tokens * PER_KEY_VALUE * heads * positions,
    )


def attend(queries, response_key_value, state, blocks, group, partial=False):
    responses, length, _ = queries.shape
    per_group = KEY_VALUE_HEADS // GROUPS
    tokens = responses * length
    width = PER_KEY_VALUE * HEAD_SIZE
    first = group * per_group
    in_specs = [pl.BlockSpec((responses, length, width), lambda i: (0, 0, first + i))]
    state_spec = pl.BlockSpec((PER_KEY_VALUE * tokens, HEAD_SIZE), lambda i: (i, 0))
    if state:
        kernel = last_kernel
        operands = state
        in_specs += [state_spec] * 2
    else:
        kernel = first_kernel if partial else whole_kernel
        operands = [response_key_value] * 2
        own = (responses, length, HEAD_SIZE)
        in_specs += [
            pl.BlockSpec(own, lambda i: (0, 0, first + i)),
            pl.BlockSpec(own, lambda i: (0, 0, KEY_VALUE_HEADS + first + i)),
        ]
    if partial:
        out_specs = [state_spec] * 2
        shape = (per_group * PER_KEY_VALUE * tokens, HEAD_SIZE)
        out_shape = [jax.ShapeDtypeStruct(shape, jnp.float32)] * 2
    else:
        out_specs = pl.BlockSpec((tokens, width), lambda i: (0, i))
        out_shape = jax.ShapeDtypeStruct((tokens, per_group * width), jnp.bfloat16)
    return pl.pallas_call(
        functools.partial(kernel, len(blocks)),
        grid=(per_group,),
        in_specs=in_specs + block_specs(blocks, first),
        out_specs=out_specs,
        out_shape=out_shape,
        compiler_params=pltpu.CompilerParams(vmem_limit_bytes=(24 if state else 60) * 1024 * 1024),
        cost_estimate=attention_cost(
            tokens, per_group, sum(block.shape[0] for block in blocks) + (0 if state else length)
        ),
    )(queries, *operands, *blocks, *blocks)


def project_kernel(sources, weight_ref, gain_ref, *refs):
    out_ref = refs[-1]
    post = gain_ref[0:1, :]
    final = gain_ref[1:2, :]
    part = weight_ref.shape[0] // GROUPS
    count = GROUPS + 1
    tokens = refs[1].shape[0]
    everything = None
    for g in range(GROUPS):
        rows = jnp.concatenate([refs[s * count + 1 + g][...] for s in range(sources)], axis=0)
        product = jnp.dot(
            rows, weight_ref[g * part : (g + 1) * part, :], preferred_element_type=jnp.float32
        )
        everything = product if g == 0 else everything + product
    for s in range(sources):
        tail_ref = refs[s * count]
        projected = everything[s * tokens : (s + 1) * tokens]
        residual = tail_ref[0:tokens, :].astype(jnp.float32)
        target = tail_ref[tokens : 2 * tokens, :].astype(jnp.float32) * final
        scaled = projected * post
        lane = lax.broadcasted_iota(jnp.int32, (tokens, 128), 1)
        packed = jnp.zeros((tokens, 128), jnp.float32)
        terms = (
            projected * projected,
            residual * scaled,
            scaled * scaled,
            target * scaled,
            residual * residual,
            residual * target,
        )
        for k, term in enumerate(terms):
            packed = jnp.where(lane == k, jnp.sum(term, axis=-1, keepdims=True), packed)
        out_ref[s] = jnp.transpose(packed)[0:SUMS, :]


def project(weight, gains, tails, attended, limit):
    sources = len(tails)
    tokens = attended[0][0].shape[0]
    width = weight.shape[1]
    operands = [weight, gains]
    for s in range(sources):
        operands += [tails[s]] + list(attended[s])
    return pl.pallas_call(
        functools.partial(project_kernel, sources),
        out_shape=jax.ShapeDtypeStruct((sources, SUMS, tokens), jnp.float32),
        compiler_params=pltpu.CompilerParams(vmem_limit_bytes=limit * 1024 * 1024),
        cost_estimate=pl.CostEstimate(
            flops=2 * sources * tokens * 2048 * width,
            bytes_accessed=8 * 1024 * 1024,
            transcendentals=0,
        ),
    )(*operands)


def body(
    queries,
    response_key_value,
    prompt_kv,
    out_weight,
    residual,
    post_gain,
    final_gain,
    target_rows,
    log_norm,
    old_logp,
    ref_logp,
    lengths,
    rewards,
):
    _, responses, length, _ = queries.shape
    tokens = responses * length
    fsdp = lax.axis_size("fsdp")
    dp = lax.axis_size("dp")
    here = lax.axis_index("fsdp")
    columns = D // fsdp

    lane = lax.broadcasted_iota(jnp.int32, (1, length), 1)
    sums = jnp.where(
        lane == 0,
        jnp.sum(rewards[0]),
        jnp.where(lane == 1, jnp.sum(lengths[0]).astype(jnp.float32), 0.0),
    )
    bit = 1

    streams = (residual[0].reshape(tokens, D), target_rows[0].reshape(tokens, D))

    def cut(k):
        start = (here ^ k) * columns
        return jnp.concatenate(
            [lax.dynamic_slice_in_dim(value, start, columns, 1) for value in streams], axis=0
        )

    tails = {}
    far = list(range(2, fsdp))

    block = prompt_kv[0]
    gathered = [block]
    rounds = dp // 2
    share = -(-len(far) // max(rounds - 2, 1))
    rows = block.shape[0]
    pieces = {key: cut(key) for key in far[:share]}
    state = None
    for step in range(rounds):
        keys = far[step * share : (step + 1) * share]
        later = far[(step + 1) * share : (step + 2) * share]
        for key in keys:
            tails[key] = swap(pieces[key], "fsdp", key)
        if step and bit < dp:
            sums = sums + swap(sums, "dp", bit)
            bit *= 2
        if step == rounds - 1:
            final_blocks = [block, crossed]
            final_blocks.append(swap(block, "dp", 1))
            sums, state = lax.optimization_barrier((sums, state))
            break
        pieces.update({key: cut(key) for key in later})
        if step == rounds - 2:
            known_blocks = list(gathered)
            state = attend(queries[0], response_key_value[0], None, gathered, 0, True)
        block, crossed = around(block, "dp"), swap(block, "dp", 1)
        behind = far[max(step - 2, 0) * share : max(step - 1, 0) * share]
        held = [tails[key] for key in behind] + [pieces[key] for key in later] + [sums]
        held += state or []
        block, crossed, *held = lax.optimization_barrier((block, crossed, *held))
        if state:
            state = held[-2:]
            held = held[:-2]
        tails.update(zip(behind, held))
        held = held[len(behind) :]
        pieces.update(zip(later, held))
        sums = held[len(later)]
        gathered += [block, crossed]
        streams, _ = lax.optimization_barrier((streams, sums))
    waiting = far[(rounds - 3) * share :]
    while bit < dp:
        sums = sums + swap(sums, "dp", bit)
        bit *= 2
    tails[0] = cut(0)
    tails[1] = swap(cut(1), "fsdp", 1)

    meta = jnp.concatenate([rewards[0], lengths[0].astype(jnp.float32), sums[0, :2]])
    meta = jnp.pad(meta[None], ((0, 0), (0, length - meta.shape[0])))
    facts = [jnp.concatenate([log_norm[0], old_logp[0], ref_logp[0], meta], axis=0)]
    bit = 1
    while bit < fsdp:
        facts = facts + [swap(value, "fsdp", bit) for value in facts]
        bit *= 2
    gains = lax.dynamic_slice_in_dim(
        jnp.stack([post_gain, final_gain]), here * columns, columns, 1
    )

    attended = [[None] * GROUPS for _ in range(fsdp)]
    asked = queries[0]
    for g in range(GROUPS):
        if g == 0:
            attended[0][g] = attend(asked, response_key_value[0], state, final_blocks, g)
        else:
            attended[0][g] = attend(
                asked, response_key_value[0], None, known_blocks + final_blocks, g
            )
        last = [tails[key] for key in waiting]
        asked, attended[0][g], *last = lax.optimization_barrier((asked, attended[0][g], *last))
        tails.update(zip(waiting, last))
        if g and fsdp > 2:
            attended[0][g], attended[fsdp // 2][g - 1] = lax.optimization_barrier(
                (attended[0][g], attended[fsdp // 2][g - 1])
            )
        bit = fsdp // 2
        known = [0]
        while bit > 1:
            for k in known:
                attended[k ^ bit][g] = swap(attended[k][g], "fsdp", bit)
            known = known + [k ^ bit for k in known]
            bit //= 2


    def project_some(some, limit):
        for k in some:
            if k & 1:
                attended[k] = [swap(value, "fsdp", 1) for value in attended[k ^ 1]]
        return project(
            out_weight,
            gains,
            [tails[k] for k in some],
            [attended[k] for k in some],
            limit,
        )

    near = project_some(list(range(min(2, fsdp))), 24)
    flat = [attended[k][-1] for k in range(2, fsdp, 2)]
    near, facts, *flat = lax.optimization_barrier((near, facts, *flat))
    for k, value in zip(range(2, fsdp, 2), flat):
        attended[k][-1] = value
    facts = jnp.stack(facts)
    parts = [near, project_some(list(range(2, fsdp)), min(6 * (fsdp - 2), 60))]
    totals = jnp.concatenate(parts, axis=0)
    bit = 1
    while bit < fsdp:
        steps = [bit, 2 * bit, 3 * bit] if 2 * bit < fsdp else [bit]
        others = [(step, swap(totals, "fsdp", step)) for step in steps]
        for step, other in others:
            totals = totals + jnp.stack([other[k ^ step] for k in range(fsdp)])
        bit *= 4

    totals = totals.reshape(fsdp, SUMS, responses, length)
    inverse = lax.rsqrt(totals[:, 0] / D + 1e-06)
    square = totals[:, 4] + inverse * (2.0 * totals[:, 1] + inverse * totals[:, 2])
    outer = lax.rsqrt(jnp.maximum(square, 0.0) / D + 1e-06)
    raw = outer * (totals[:, 5] + inverse * totals[:, 3])
    logit = 30.0 * jnp.tanh(raw / 30.0)
    logp = logit - facts[:, 0:responses]
    old = facts[:, responses : 2 * responses]
    ref = facts[:, 2 * responses : 3 * responses]
    meta = facts[:, 3 * responses]
    group_sum = meta[:, 2 * responses]
    group_count = meta[:, 2 * responses + 1]
    reward = meta[:, :responses]
    size = meta[:, responses : 2 * responses].astype(jnp.int32)
    position = lax.broadcasted_iota(jnp.int32, (fsdp, responses, length), 2)
    live = position < size[:, :, None]
    log_ratio = jnp.where(live, logp - old, 0.0)
    drift = ref - logp
    kl_terms = jnp.where(live, jnp.exp(drift) - drift - 1.0, 0.0)
    advantage = (reward - (group_sum / (responses * dp))[:, None])[:, :, None]
    ratio = jnp.exp(logp - old)
    surrogate = jnp.minimum(ratio * advantage, jnp.clip(ratio, 0.8, 1.2) * advantage)
    objective = jnp.where(live, 0.04 * kl_terms - surrogate, 0.0)
    loss = jnp.sum(objective, axis=(0, 1))[None]
    bit = 1
    while bit < dp:
        steps = [bit, 2 * bit, 3 * bit] if 1 < bit and 2 * bit < dp else [bit]
        loss = sum([swap(loss, "dp", step) for step in steps], loss)
        bit *= 4 if len(steps) > 1 else 2
    batch_loss = jnp.sum(loss) / jnp.sum(group_count)
    return (log_ratio[:1], kl_terms[:1], objective[:1], batch_loss)


def solution(mesh):
    rows4 = P("fsdp", "dp", None, None)
    rows3 = P("fsdp", "dp", None)
    in_specs = (
        rows4,
        rows4,
        rows3,
        P(None, "fsdp"),
        rows4,
        P(),
        P(),
        rows4,
        rows3,
        rows3,
        rows3,
        P("fsdp", "dp"),
        P("fsdp", "dp"),
    )
    out_specs = (rows3, rows3, rows3, P())
    return jax.shard_map(body, mesh=mesh, in_specs=in_specs, out_specs=out_specs, check_vma=False)
```

```python
import functools
import math

import jax
import jax.numpy as jnp
from jax import lax
from jax.experimental import pallas as pl
from jax.experimental.pallas import tpu as pltpu
from jax.sharding import PartitionSpec as P

D = 4608
KEY_VALUE_HEADS = 8
PER_KEY_VALUE = 2
HEAD_SIZE = 128
QPRE = 144
GROUPS = 2
CHUNK = 512
SUMS = 8


def swap(value, axis, bit):
    count = lax.axis_size(axis)
    return lax.ppermute(value, axis, [(i, i ^ bit) for i in range(count)])


def around(value, axis):
    half = lax.axis_size(axis) // 2
    order = list(range(0, half, 2)) + list(range(1, half, 2))[::-1]
    after = {order[i]: order[(i + 1) % half] for i in range(half)}
    return lax.ppermute(
        value, axis, [(i, after[i // 2] * 2 + i % 2) for i in range(2 * half)]
    )


def weigh(q_rows, k_rows):
    scores = lax.dot_general(
        q_rows, k_rows, (((1,), (1,)), ((), ())), preferred_element_type=jnp.float32
    )
    return jnp.exp2(50.0 * math.log2(math.e) * jnp.tanh(scores * (QPRE**-0.5 / 50.0)))


def stacked(q_ref):
    responses, length, _ = q_ref.shape
    q = q_ref[...].reshape(responses * length, PER_KEY_VALUE * HEAD_SIZE)
    return jnp.concatenate(
        [q[:, h * HEAD_SIZE : (h + 1) * HEAD_SIZE] for h in range(PER_KEY_VALUE)], axis=0
    )


def gather_in(stack, key_refs, value_refs, numerator, total):
    keys = jnp.concatenate([ref[...] for ref in key_refs], axis=0)
    values = jnp.concatenate([ref[...] for ref in value_refs], axis=0)
    count = keys.shape[0]
    for start in range(0, count, CHUNK):
        stop = min(start + CHUNK, count)
        weights = weigh(stack, keys[start:stop])
        for lane in range(0, stop - start, HEAD_SIZE):
            piece = weights[:, lane : lane + HEAD_SIZE]
            if piece.shape[1] < HEAD_SIZE:
                piece = jnp.pad(piece, ((0, 0), (0, HEAD_SIZE - piece.shape[1])))
            total = total + piece
        numerator = numerator + jnp.dot(
            weights.astype(jnp.bfloat16), values[start:stop], preferred_element_type=jnp.float32
        )
    return numerator, total


def begin(q_ref, rk_ref, rv_ref, key_refs, value_refs):
    responses, length, _ = q_ref.shape
    later = lax.broadcasted_iota(jnp.int32, (length, length), 0)
    earlier = lax.broadcasted_iota(jnp.int32, (length, length), 1)
    causal = earlier <= later
    stack = stacked(q_ref)
    owned, numerators = [], []
    for i in range(PER_KEY_VALUE * responses):
        r = i % responses
        own = jnp.where(causal, weigh(stack[i * length : (i + 1) * length], rk_ref[r]), 0.0)
        owned.append(own)
        numerators.append(
            jnp.dot(own.astype(jnp.bfloat16), rv_ref[r], preferred_element_type=jnp.float32)
        )
    return gather_in(
        stack,
        key_refs,
        value_refs,
        jnp.concatenate(numerators, axis=0),
        jnp.concatenate(owned, axis=0),
    )


def finish(tokens, numerator, total, out_ref):
    result = (numerator / jnp.sum(total, axis=-1, keepdims=True)).astype(jnp.bfloat16)
    for h in range(PER_KEY_VALUE):
        out_ref[:, h * HEAD_SIZE : (h + 1) * HEAD_SIZE] = result[h * tokens : (h + 1) * tokens]


def first_kernel(count, q_ref, rk_ref, rv_ref, *refs):
    numerator, total = begin(q_ref, rk_ref, rv_ref, refs[:count], refs[count : 2 * count])
    refs[-2][...] = numerator
    refs[-1][...] = total


def whole_kernel(count, q_ref, rk_ref, rv_ref, *refs):
    tokens = q_ref.shape[0] * q_ref.shape[1]
    numerator, total = begin(q_ref, rk_ref, rv_ref, refs[:count], refs[count : 2 * count])
    finish(tokens, numerator, total, refs[-1])


def last_kernel(count, q_ref, numerator_ref, total_ref, *refs):
    key_refs, value_refs, out_ref = refs[:count], refs[count : 2 * count], refs[-1]
    tokens = q_ref.shape[0] * q_ref.shape[1]
    numerator, total = gather_in(
        stacked(q_ref), key_refs, value_refs, numerator_ref[...], total_ref[...]
    )
    finish(tokens, numerator, total, out_ref)


def block_specs(blocks, first):
    return [
        pl.BlockSpec((block.shape[0], HEAD_SIZE), lambda i, offset=offset: (0, offset + i))
        for offset in (first, KEY_VALUE_HEADS + first)
        for block in blocks
    ]


def attention_cost(tokens, heads, positions):
    return pl.CostEstimate(
        flops=2 * 2 * tokens * PER_KEY_VALUE * heads * positions * HEAD_SIZE,
        bytes_accessed=4 * 1024 * 1024,
        transcendentals=2 * tokens * PER_KEY_VALUE * heads * positions,
    )


def attend(queries, response_key_value, state, blocks, group, partial=False):
    responses, length, _ = queries.shape
    per_group = KEY_VALUE_HEADS // GROUPS
    tokens = responses * length
    width = PER_KEY_VALUE * HEAD_SIZE
    first = group * per_group
    in_specs = [pl.BlockSpec((responses, length, width), lambda i: (0, 0, first + i))]
    state_spec = pl.BlockSpec((PER_KEY_VALUE * tokens, HEAD_SIZE), lambda i: (i, 0))
    if state:
        kernel = last_kernel
        operands = state
        in_specs += [state_spec] * 2
    else:
        kernel = first_kernel if partial else whole_kernel
        operands = [response_key_value] * 2
        own = (responses, length, HEAD_SIZE)
        in_specs += [
            pl.BlockSpec(own, lambda i: (0, 0, first + i)),
            pl.BlockSpec(own, lambda i: (0, 0, KEY_VALUE_HEADS + first + i)),
        ]
    if partial:
        out_specs = [state_spec] * 2
        shape = (per_group * PER_KEY_VALUE * tokens, HEAD_SIZE)
        out_shape = [jax.ShapeDtypeStruct(shape, jnp.float32)] * 2
    else:
        out_specs = pl.BlockSpec((tokens, width), lambda i: (0, i))
        out_shape = jax.ShapeDtypeStruct((tokens, per_group * width), jnp.bfloat16)
    return pl.pallas_call(
        functools.partial(kernel, len(blocks)),
        grid=(per_group,),
        in_specs=in_specs + block_specs(blocks, first),
        out_specs=out_specs,
        out_shape=out_shape,
        compiler_params=pltpu.CompilerParams(vmem_limit_bytes=(24 if state else 60) * 1024 * 1024),
        cost_estimate=attention_cost(
            tokens, per_group, sum(block.shape[0] for block in blocks) + (0 if state else length)
        ),
    )(queries, *operands, *blocks, *blocks)


def project_kernel(sources, weight_ref, gain_ref, *refs):
    out_ref = refs[-1]
    post = gain_ref[0:1, :]
    final = gain_ref[1:2, :]
    part = weight_ref.shape[0] // GROUPS
    count = GROUPS + 1
    tokens = refs[1].shape[0]
    everything = None
    for g in range(GROUPS):
        rows = jnp.concatenate([refs[s * count + 1 + g][...] for s in range(sources)], axis=0)
        product = jnp.dot(
            rows, weight_ref[g * part : (g + 1) * part, :], preferred_element_type=jnp.float32
        )
        everything = product if g == 0 else everything + product
    for s in range(sources):
        tail_ref = refs[s * count]
        projected = everything[s * tokens : (s + 1) * tokens]
        residual = tail_ref[0:tokens, :].astype(jnp.float32)
        target = tail_ref[tokens : 2 * tokens, :].astype(jnp.float32) * final
        scaled = projected * post
        lane = lax.broadcasted_iota(jnp.int32, (tokens, 128), 1)
        packed = jnp.zeros((tokens, 128), jnp.float32)
        terms = (
            projected * projected,
            residual * scaled,
            scaled * scaled,
            target * scaled,
            residual * residual,
            residual * target,
        )
        for k, term in enumerate(terms):
            packed = jnp.where(lane == k, jnp.sum(term, axis=-1, keepdims=True), packed)
        out_ref[s] = jnp.transpose(packed)[0:SUMS, :]


def project(weight, gains, tails, attended, limit):
    sources = len(tails)
    tokens = attended[0][0].shape[0]
    width = weight.shape[1]
    operands = [weight, gains]
    for s in range(sources):
        operands += [tails[s]] + list(attended[s])
    return pl.pallas_call(
        functools.partial(project_kernel, sources),
        out_shape=jax.ShapeDtypeStruct((sources, SUMS, tokens), jnp.float32),
        compiler_params=pltpu.CompilerParams(vmem_limit_bytes=limit * 1024 * 1024),
        cost_estimate=pl.CostEstimate(
            flops=2 * sources * tokens * 2048 * width,
            bytes_accessed=8 * 1024 * 1024,
            transcendentals=0,
        ),
    )(*operands)


def body(
    queries,
    response_key_value,
    prompt_kv,
    out_weight,
    residual,
    post_gain,
    final_gain,
    target_rows,
    log_norm,
    old_logp,
    ref_logp,
    lengths,
    rewards,
):
    _, responses, length, _ = queries.shape
    tokens = responses * length
    fsdp = lax.axis_size("fsdp")
    dp = lax.axis_size("dp")
    here = lax.axis_index("fsdp")
    columns = D // fsdp

    lane = lax.broadcasted_iota(jnp.int32, (1, length), 1)
    sums = jnp.where(
        lane == 0,
        jnp.sum(rewards[0]),
        jnp.where(lane == 1, jnp.sum(lengths[0]).astype(jnp.float32), 0.0),
    )
    bit = 1

    streams = (residual[0].reshape(tokens, D), target_rows[0].reshape(tokens, D))

    def cut(k):
        start = (here ^ k) * columns
        return jnp.concatenate(
            [lax.dynamic_slice_in_dim(value, start, columns, 1) for value in streams], axis=0
        )

    tails = {}
    far = list(range(2, fsdp))

    block = prompt_kv[0]
    gathered = [block]
    rounds = dp // 2
    share = -(-len(far) // max(rounds - 2, 1))
    rows = block.shape[0]
    pieces = {key: cut(key) for key in far[:share]}
    state = None
    for step in range(rounds):
        keys = far[step * share : (step + 1) * share]
        later = far[(step + 1) * share : (step + 2) * share]
        for key in keys:
            tails[key] = swap(pieces[key], "fsdp", key)
        if step and bit < dp:
            sums = sums + swap(sums, "dp", bit)
            bit *= 2
        if step == rounds - 1:
            final_blocks = [block, crossed]
            final_blocks.append(swap(block, "dp", 1))
            sums, state = lax.optimization_barrier((sums, state))
            break
        pieces.update({key: cut(key) for key in later})
        if step == rounds - 2:
            known_blocks = list(gathered)
            state = attend(queries[0], response_key_value[0], None, gathered, 0, True)
        block, crossed = around(block, "dp"), swap(block, "dp", 1)
        behind = far[max(step - 2, 0) * share : max(step - 1, 0) * share]
        held = [tails[key] for key in behind] + [pieces[key] for key in later] + [sums]
        held += state or []
        block, crossed, *held = lax.optimization_barrier((block, crossed, *held))
        if state:
            state = held[-2:]
            held = held[:-2]
        tails.update(zip(behind, held))
        held = held[len(behind) :]
        pieces.update(zip(later, held))
        sums = held[len(later)]
        gathered += [block, crossed]
        streams, _ = lax.optimization_barrier((streams, sums))
    waiting = far[(rounds - 3) * share :]
    while bit < dp:
        sums = sums + swap(sums, "dp", bit)
        bit *= 2
    tails[0] = cut(0)
    tails[1] = swap(cut(1), "fsdp", 1)

    meta = jnp.concatenate([rewards[0], lengths[0].astype(jnp.float32), sums[0, :2]])
    meta = jnp.pad(meta[None], ((0, 0), (0, length - meta.shape[0])))
    facts = [jnp.concatenate([log_norm[0], old_logp[0], ref_logp[0], meta], axis=0)]
    bit = 1
    while bit < fsdp:
        facts = facts + [swap(value, "fsdp", bit) for value in facts]
        bit *= 2
    gains = lax.dynamic_slice_in_dim(
        jnp.stack([post_gain, final_gain]), here * columns, columns, 1
    )

    attended = [[None] * GROUPS for _ in range(fsdp)]
    asked = queries[0]
    for g in range(GROUPS):
        if g == 0:
            attended[0][g] = attend(asked, response_key_value[0], state, final_blocks, g)
        else:
            attended[0][g] = attend(
                asked, response_key_value[0], None, known_blocks + final_blocks, g
            )
        last = [tails[key] for key in waiting]
        asked, attended[0][g], *last = lax.optimization_barrier((asked, attended[0][g], *last))
        tails.update(zip(waiting, last))
        bit = fsdp // 2
        known = [0]
        while bit > 1:
            for k in known:
                attended[k ^ bit][g] = swap(attended[k][g], "fsdp", bit)
            known = known + [k ^ bit for k in known]
            bit //= 2


    def project_some(some, limit):
        for k in some:
            if k & 1:
                attended[k] = [swap(value, "fsdp", 1) for value in attended[k ^ 1]]
        return project(
            out_weight,
            gains,
            [tails[k] for k in some],
            [attended[k] for k in some],
            limit,
        )

    near = project_some(list(range(min(2, fsdp))), 24)
    flat = [attended[k][-1] for k in range(2, fsdp, 2)]
    near, facts, *flat = lax.optimization_barrier((near, facts, *flat))
    for k, value in zip(range(2, fsdp, 2), flat):
        attended[k][-1] = value
    facts = jnp.stack(facts)
    parts = [near, project_some(list(range(2, fsdp)), min(6 * (fsdp - 2), 60))]
    totals = jnp.concatenate(parts, axis=0)
    bit = 1
    while bit < fsdp:
        steps = [bit, 2 * bit, 3 * bit] if 2 * bit < fsdp else [bit]
        others = [(step, swap(totals, "fsdp", step)) for step in steps]
        for step, other in others:
            totals = totals + jnp.stack([other[k ^ step] for k in range(fsdp)])
        bit *= 4

    totals = totals.reshape(fsdp, SUMS, responses, length)
    inverse = lax.rsqrt(totals[:, 0] / D + 1e-06)
    square = totals[:, 4] + inverse * (2.0 * totals[:, 1] + inverse * totals[:, 2])
    outer = lax.rsqrt(jnp.maximum(square, 0.0) / D + 1e-06)
    raw = outer * (totals[:, 5] + inverse * totals[:, 3])
    logit = 30.0 * jnp.tanh(raw / 30.0)
    logp = logit - facts[:, 0:responses]
    old = facts[:, responses : 2 * responses]
    ref = facts[:, 2 * responses : 3 * responses]
    meta = facts[:, 3 * responses]
    group_sum = meta[:, 2 * responses]
    group_count = meta[:, 2 * responses + 1]
    reward = meta[:, :responses]
    size = meta[:, responses : 2 * responses].astype(jnp.int32)
    position = lax.broadcasted_iota(jnp.int32, (fsdp, responses, length), 2)
    live = position < size[:, :, None]
    log_ratio = jnp.where(live, logp - old, 0.0)
    drift = ref - logp
    kl_terms = jnp.where(live, jnp.exp(drift) - drift - 1.0, 0.0)
    advantage = (reward - (group_sum / (responses * dp))[:, None])[:, :, None]
    ratio = jnp.exp(logp - old)
    surrogate = jnp.minimum(ratio * advantage, jnp.clip(ratio, 0.8, 1.2) * advantage)
    objective = jnp.where(live, 0.04 * kl_terms - surrogate, 0.0)
    loss = jnp.sum(objective, axis=(0, 1))[None]
    bit = 1
    while bit < dp:
        steps = [bit, 2 * bit, 3 * bit] if 1 < bit and 2 * bit < dp else [bit]
        loss = sum([swap(loss, "dp", step) for step in steps], loss)
        bit *= 4 if len(steps) > 1 else 2
    batch_loss = jnp.sum(loss) / jnp.sum(group_count)
    return (log_ratio[:1], kl_terms[:1], objective[:1], batch_loss)


def solution(mesh):
    rows4 = P("fsdp", "dp", None, None)
    rows3 = P("fsdp", "dp", None)
    in_specs = (
        rows4,
        rows4,
        rows3,
        P(None, "fsdp"),
        rows4,
        P(),
        P(),
        rows4,
        rows3,
        rows3,
        rows3,
        P("fsdp", "dp"),
        P("fsdp", "dp"),
    )
    out_specs = (rows3, rows3, rows3, P())
    return jax.shard_map(body, mesh=mesh, in_specs=in_specs, out_specs=out_specs, check_vma=False)
```
